32 devices in a mesh: seq: 8 (over z, x), win: 4 (over y, core).
Axes of the slice: x: 2, y: 2, z: 4, core: 2. Of those that a mesh axis runs over, the one named last changes fastest.
Arguments:
- inputs: bfloat16 [16, 1024, 1024], P('win', 'seq'), may hold values from -6 to 6
- cotangent: bfloat16 [16, 1024, 1024], P('win', 'seq'), may hold values from -6 to 6
- offsets: int32 [16], P('win'), may hold values from 1 to 1023
- end_flags: int32 [16], P('win'), may hold values from 0 to 1, as said below
- ln_gain: float32 [1024], replicated, may hold values from 0.1 to 1.9
- ln_bias: float32 [1024], replicated, may hold values from -1.75 to 1.75
- w_query: bfloat16 [1024, 1024], replicated, may hold values from -0.1875 to 0.1875
- w_key: bfloat16 [1024, 1024], replicated, may hold values from -0.1875 to 0.1875
- w_value: bfloat16 [1024, 1024], replicated, may hold values from -0.1875 to 0.1875
- w_proj: bfloat16 [1024, 1024], replicated, may hold values from -2 to 2
- w_in: bfloat16 [1024, 4096], replicated, may hold values from -0.1875 to 0.1875
- b_in: float32 [4096], replicated, may hold values from -3 to 3
- w_out: bfloat16 [4096, 1024], replicated, may hold values from -0.09375 to 0.09375
- b_out: float32 [1024], replicated, may hold values from -1.75 to 1.75
Outputs:
- outputs: bfloat16 [16, 1024, 1024], P('win', 'seq')
- grad_inputs: float32 [16, 1024, 1024], P('win', 'seq')
- grad_ln_gain: float32 [1024], replicated
- grad_ln_bias: float32 [1024], replicated
- grad_w_query: float32 [1024, 1024], replicated
- grad_w_key: float32 [1024, 1024], replicated
- grad_w_value: float32 [1024, 1024], replicated
- grad_w_proj: float32 [1024, 1024], replicated
- grad_w_in: float32 [1024, 4096], replicated
- grad_b_in: float32 [4096], replicated
- grad_w_out: float32 [4096, 1024], replicated
- grad_b_out: float32 [1024], replicated
The draws below stay inside these ranges and needn't reach their ends.
Inputs may be any that keep to these rules, and one draw needn't show every extreme that they name: `end_flags`: in each block of 4 consecutive windows at least one window has flag 0.
All inputs are finite; a program needn't handle non-finite values.
Results may differ from the reference program's by a relative error of at most 0.012.
Values may be sent and summed in bfloat16 or wider, within the bound.
No kernel may reach another device: no remote copies, remote signals or barrier semaphores. Data moves between devices by JAX's collectives and lax.ppermute only.
A program may use at most 320 MiB of HBM per device.

```python
import math
import jax
import jax.numpy as jnp
from jax import lax

D = 1024
HEADS = 16
HEAD_DIM = 64
ROT = 32
FF = 4096
LEN = 1024
WIN_DEV = 4
WINDOWS = 16


def draw_end_flags(key, part):
    key = jax.random.fold_in(key, 7)
    coin_key, pick_key = jax.random.split(key)
    coin_bits = jax.random.randint(coin_key, (WINDOWS,), 0, 2)
    picked = jax.random.randint(pick_key, (WINDOWS // WIN_DEV,), 0, WIN_DEV)
    window_index = jnp.arange(WINDOWS)
    chosen = picked[window_index // WIN_DEV]
    return jnp.where(window_index % WIN_DEV == chosen, 0, coin_bits).astype(jnp.int32)


def with_ends(array, stream_key, smallest, top_value):
    index_at = [jax.random.randint(jax.random.fold_in(stream_key, axis), (), 0, length) for axis, length in enumerate(array.shape)]
    longest = array.shape.index(max(array.shape))
    neighbour = index_at[:longest] + [(index_at[longest] + 1) % array.shape[longest]] + index_at[longest + 1:]
    return array.at[tuple(index_at)].set(smallest).at[tuple(neighbour)].set(top_value)


def block_levels(stream_key, shape, shards, smallest, high):
    level, own = 1.0, jax.random.fold_in(stream_key, 6)
    for dim, parts in shards:
        steps = jnp.exp(jax.random.uniform(jax.random.fold_in(own, dim), (parts,), jnp.float32, smallest / len(shards), high / len(shards)))
        level = level * jnp.repeat(steps, shape[dim] // parts).reshape([-1 if axis == dim else 1 for axis in range(len(shape))])
    return level


def scatter_about(key, extent, scale, limit, cuts=(), held_as=jnp.bfloat16):
    level = block_levels(key, extent, cuts, -0.22, 0.18) if cuts else 1.0
    values = jax.random.normal(key, extent, jnp.float32) * scale * level
    return jnp.minimum(jnp.maximum(values, -limit), limit).astype(held_as)


def setup_inputs(seed: int = 0) -> dict:
    key_of = jax.random.split(jax.random.key(seed), 15)
    return {
        "inputs": scatter_about(key_of[0], (WINDOWS, LEN, D), 1.0, 6.0, ((0, 4), (1, 8))),
        "cotangent": scatter_about(key_of[1], (WINDOWS, LEN, D), 1.0, 6.0, ((0, 4), (1, 8))),
        "offsets": with_ends(jax.random.randint(key_of[2], (WINDOWS,), 1, LEN), jax.random.fold_in(key_of[2], 1), 1, LEN - 1).astype(jnp.int32),
        "end_flags": draw_end_flags(jax.random.fold_in(key_of[14], 71), 0),
        "ln_gain": jnp.clip(1.0 + 0.18 * jax.random.normal(key_of[4], (D,), jnp.float32), 0.1, 1.9),
        "ln_bias": scatter_about(key_of[5], (D,), 0.3, 1.75, (), jnp.float32),
        "w_query": scatter_about(key_of[6], (D, D), D ** -0.5, 0.1875),
        "w_key": scatter_about(key_of[7], (D, D), D ** -0.5, 0.1875),
        "w_value": scatter_about(key_of[8], (D, D), D ** -0.5, 0.1875),
        "w_proj": scatter_about(key_of[9], (D, D), (max(D // 128, 1)) ** -0.5, 2.0),
        "w_in": scatter_about(key_of[10], (D, FF), D ** -0.5, 0.1875),
        "b_in": scatter_about(key_of[11], (FF,), 0.5, 3.0, (), jnp.float32),
        "w_out": scatter_about(key_of[12], (FF, D), FF ** -0.5, 0.09375),
        "b_out": scatter_about(key_of[13], (D,), 0.3, 1.75, (), jnp.float32),
    }


@jax.custom_vjp
def low(v):
    return lax.optimization_barrier(v.astype(jnp.bfloat16)).astype(jnp.float32)

@jax.custom_vjp
def low_back(v):
    return v

def low_keep(v):
    return (low(v), None)

def low_pass(kept, grad):
    return (grad,)

def back_keep(v):
    return (v, None)

def back_low(kept, grad):
    return (low(grad),)
low.defvjp(low_keep, low_pass)
low_back.defvjp(back_keep, back_low)

def tables(count, model_width, head_width, rot_width, first_row):
    position = (first_row + jnp.arange(count)).astype(jnp.float32)
    column = jnp.arange(model_width) % head_width
    pair_index = (column // 2).astype(jnp.float32)
    frequency = jnp.exp(pair_index * (-2.0 * math.log(10000.0) / rot_width))
    angles = position[:, None] * frequency[None, :]
    rotated = column < rot_width
    is_even = column % 2 == 0
    cosine = jnp.where(rotated, jnp.cos(angles), 1.0)
    sine = jnp.where(rotated, jnp.sin(angles), 0.0)
    ahead = jnp.where(is_even, -sine, 0.0)
    behind = jnp.where(is_even, 0.0, sine)
    return (cosine, ahead, behind)

def rotate(values, cosine, ahead, behind):
    return values * cosine + jnp.roll(values, -1, axis=-1) * ahead + jnp.roll(values, 1, axis=-1) * behind

def layernorm(values, gain, shift):
    center = values - lax.optimization_barrier(jnp.mean(values, axis=-1, keepdims=True))
    spread = lax.optimization_barrier(jnp.mean(center * center, axis=-1, keepdims=True))
    return center * lax.rsqrt(spread + 1e-05) * gain + shift

def attend_window(packed):
    query, keys, values, bound = packed
    count = query.shape[0]
    highest = lax.Precision.HIGHEST
    q_heads = query.reshape(count, HEADS, HEAD_DIM)
    k_heads = keys.reshape(count, HEADS, HEAD_DIM)
    v_heads = values.reshape(count, HEADS, HEAD_DIM)
    raw_scores = jnp.einsum('qhd,khd->hqk', q_heads, k_heads, precision=highest) * HEAD_DIM ** (-0.5)
    row_index = jnp.arange(count)[:, None]
    col_index = jnp.arange(count)[None, :]
    allowed = (col_index <= row_index) & ((row_index >= bound) == (col_index >= bound))
    scores = low_back(jnp.where(allowed[None], raw_scores, -1e+30))
    probs = jax.nn.softmax(scores, axis=-1)
    mixed = jnp.einsum('hqk,khd->qhd', low(probs), v_heads, precision=highest)
    return mixed.reshape(count, HEADS * HEAD_DIM)

def project(normed, weight):
    return jnp.einsum('gnd,de->gne', normed, weight, precision=lax.Precision.HIGHEST)

def layer_block(states, ln_gain, ln_bias, w_query, w_key, w_value, w_proj, w_in, b_in, w_out, b_out, bounds, cosine, ahead, behind):
    normed = low(layernorm(states, ln_gain, ln_bias))
    query = low_back(low(rotate(low_back(project(normed, w_query)), cosine, ahead, behind)))
    keys = low_back(low(rotate(low_back(project(normed, w_key)), cosine, ahead, behind)))
    values = low_back(low(project(normed, w_value)))
    heads_out = lax.map(jax.checkpoint(attend_window), (query, keys, values, bounds))
    mixed = low_back(low(heads_out))
    attended = project(mixed, w_proj)
    inner = low_back(project(normed, w_in) + b_in)
    activated = low(jax.nn.gelu(inner, approximate=True))
    return states + attended + project(activated, w_out) + b_out

def reference(inputs, cotangent, offsets, end_flags, ln_gain, ln_bias, w_query, w_key, w_value, w_proj, w_in, b_in, w_out, b_out):
    group_size = min(WINDOWS, max(1, 4096 // LEN))
    while WINDOWS % group_size:
        group_size -= 1
    groups = WINDOWS // group_size
    bounds = jnp.where(end_flags == 1, offsets, 0).astype(jnp.int32)
    params = tuple((member.astype(jnp.float32) for member in (ln_gain, ln_bias, w_query, w_key, w_value, w_proj, w_in, b_in, w_out, b_out)))
    cosine, ahead, behind = tables(LEN, D, HEAD_DIM, ROT, 0)
    states_all = inputs.astype(jnp.float32).reshape(groups, group_size, LEN, D)
    cots_all = cotangent.astype(jnp.float32).reshape(groups, group_size, LEN, D)
    bounds_all = bounds.reshape(groups, group_size)

    def scan_body(summed, packed):
        states, cots, group_bounds = packed

        def forward(values, *weights):
            return layer_block(values, *weights, group_bounds, cosine, ahead, behind)
        result, backward = jax.vjp(forward, states, *params)
        grads = backward(cots)
        summed = tuple((accum + member for accum, member in zip(summed, grads[1:])))
        return (summed, (result.astype(jnp.bfloat16), grads[0]))
    initial = tuple((jnp.zeros_like(member) for member in params))
    summed, (results, grad_states) = lax.scan(scan_body, initial, (states_all, cots_all, bounds_all))
    return (results.reshape(WINDOWS, LEN, D), grad_states.reshape(WINDOWS, LEN, D), summed[0], summed[1], summed[2], summed[3], summed[4], summed[5], summed[6], summed[7], summed[8], summed[9])
```

```python
import functools
import math

import jax
import jax.numpy as jnp
from jax import lax
from jax.experimental import pallas as pl
from jax.experimental.pallas import tpu as pltpu
from jax.sharding import PartitionSpec as P

HEAD_DIM = 64
ROT = 32
LANES = 128
BF = jnp.bfloat16
F32 = jnp.float32


def tables(count, model_width, head_width, rot_width, first_row):
    position = (first_row + jnp.arange(count)).astype(F32)
    column = jnp.arange(model_width) % head_width
    pair_index = (column // 2).astype(F32)
    frequency = jnp.exp(pair_index * (-2.0 * math.log(10000.0) / rot_width))
    angles = position[:, None] * frequency[None, :]
    rotated = column < rot_width
    is_even = column % 2 == 0
    cosine = jnp.where(rotated, jnp.cos(angles), 1.0)
    sine = jnp.where(rotated, jnp.sin(angles), 0.0)
    ahead = jnp.where(is_even, -sine, 0.0)
    behind = jnp.where(is_even, 0.0, sine)
    return (cosine, ahead, behind)


def layernorm(values, gain, shift):
    center = values - jnp.mean(values, axis=-1, keepdims=True)
    spread = jnp.mean(center * center, axis=-1, keepdims=True)
    return center * lax.rsqrt(spread + 1e-05) * gain + shift


def gelu_tanh(values):
    return jax.nn.gelu(values, approximate=True)


def dot(left, right, left_dim=1, right_dim=0):
    return lax.dot_general(
        left, right, (((left_dim,), (right_dim,)), ((), ())), preferred_element_type=F32
    )


def attention_kernel(
    bound_ref, q_ref, k_ref, v_ref, g_ref, cos_ref, ahead_ref, behind_ref,
    mixed_ref, gq_ref, gk_ref, gv_ref,
    k_turned, v_turned, mixed_turned, gq_turned, gk_sum, gv_sum, *, block,
):
    count, lanes = q_ref.shape
    bound = bound_ref[0]
    cosine, ahead, behind = cos_ref[...], ahead_ref[...], behind_ref[...]

    def rotate(values):
        return (
            values * cosine
            + pltpu.roll(values, lanes - 1, 1) * ahead
            + pltpu.roll(values, 1, 1) * behind
        )

    def rotate_back(grads):
        return (
            grads * cosine
            + pltpu.roll(grads * ahead, 1, 1)
            + pltpu.roll(grads * behind, lanes - 1, 1)
        )

    query = (rotate(q_ref[...]).astype(BF).astype(F32) * HEAD_DIM ** -0.5).astype(BF)
    key = rotate(k_ref[...]).astype(BF)
    value = v_ref[...]
    grad = g_ref[...]
    k_turned[...] = key.T
    v_turned[...] = value.T
    gk_sum[...] = jnp.zeros_like(gk_sum)
    gv_sum[...] = jnp.zeros_like(gv_sum)
    lane = lax.broadcasted_iota(jnp.int32, (count, lanes), 1)
    for head in range(lanes // HEAD_DIM):
        cols = slice(head * HEAD_DIM, (head + 1) * HEAD_DIM)
        mine = (lane >= head * HEAD_DIM) & (lane < (head + 1) * HEAD_DIM)
        q_head = jnp.where(mine, query, jnp.zeros_like(query))
        g_head = jnp.where(mine, grad, jnp.zeros_like(grad))
        for start in range(0, count, block):
            seen = start + block
            rows = slice(start, seen)
            scores = dot(key[:seen], q_head[rows], 1, 1)
            at_key = lax.broadcasted_iota(jnp.int32, (seen, block), 0)
            at_query = lax.broadcasted_iota(jnp.int32, (1, block), 1) + start
            lowest = jnp.where(at_query >= bound, bound, 0)
            scores = jnp.where((at_key <= at_query) & (at_key >= lowest), scores, -1e30)
            probs = jnp.exp(scores - jnp.max(scores, axis=0, keepdims=True))
            probs = probs * (1.0 / jnp.sum(probs, axis=0, keepdims=True))
            probs_low = probs.astype(BF)
            grad_probs = dot(value[:seen], g_head[rows], 1, 1)
            row_dot = jnp.sum(probs * grad_probs, axis=0, keepdims=True)
            grad_scores = (probs * (grad_probs - row_dot)).astype(BF)
            mixed_turned[cols, rows] = dot(v_turned[cols, :seen], probs_low)
            gq_turned[cols, rows] = dot(k_turned[cols, :seen], grad_scores)
            gv_sum[:seen, :] += dot(probs_low, g_head[rows])
            gk_sum[:seen, :] += dot(grad_scores, q_head[rows])
    mixed_ref[...] = mixed_turned[...].T.astype(BF)
    grad_query = (gq_turned[...].T * HEAD_DIM ** -0.5).astype(BF).astype(F32)
    gq_ref[...] = rotate_back(grad_query).astype(BF)
    gk_ref[...] = rotate_back(gk_sum[...].astype(BF).astype(F32)).astype(BF)
    gv_ref[...] = gv_sum[...].astype(BF)


def attention(bound, query_raw, key_raw, value, grad_mixed, turns):
    count, width = query_raw.shape
    cols = pl.BlockSpec((count, LANES), lambda pair, bound: (0, pair))
    table = pl.BlockSpec((count, LANES), lambda pair, bound: (0, 0))
    return pl.pallas_call(
        functools.partial(attention_kernel, block=512),
        grid_spec=pltpu.PrefetchScalarGridSpec(
            num_scalar_prefetch=1,
            grid=(width // LANES,),
            in_specs=[cols] * 4 + [table] * 3,
            out_specs=[cols] * 4,
            scratch_shapes=[pltpu.VMEM((LANES, count), BF)] * 2
            + [pltpu.VMEM((LANES, count), F32)] * 2
            + [pltpu.VMEM((count, LANES), F32)] * 2,
        ),
        out_shape=[jax.ShapeDtypeStruct((count, width), BF)] * 4,
        compiler_params=pltpu.CompilerParams(vmem_limit_bytes=48 << 20),
        cost_estimate=pl.CostEstimate(
            flops=6 * 2 * count * count * width,
            bytes_accessed=20 * count * width,
            transcendentals=count * count * width // HEAD_DIM,
        ),
    )(bound.reshape(1), query_raw, key_raw, value, grad_mixed, *turns)


def swap(values, axis, bits):
    return lax.ppermute(
        values, axis, [(i, i ^ bits) for i in range(lax.axis_size(axis))]
    )


def cross(values):
    n_seq, n_win = lax.axis_size("seq"), lax.axis_size("win")
    pairs = []
    for s in range(n_seq):
        for w in range(n_win):
            s_to, w_to = (s & ~1) | (w & 1), (w & ~1) | (s & 1)
            pairs.append((s * n_win + w, s_to * n_win + w_to))
    return lax.ppermute(values, ("seq", "win"), pairs)


def trade_z(cube, z):
    count = cube.shape[0]
    own = lax.dynamic_index_in_dim(cube, z, 0, keepdims=True)
    out = lax.dynamic_update_slice_in_dim(jnp.zeros_like(cube), own, z, 0)
    for k in range(1, count):
        sent = lax.dynamic_index_in_dim(cube, z ^ k, 0, keepdims=True)
        out = lax.dynamic_update_slice_in_dim(out, swap(sent, "seq", 2 * k), z ^ k, 0)
    return out


def ordered(first_is_own, own, other, axis):
    return jnp.where(
        first_is_own,
        jnp.concatenate([own, other], axis=axis),
        jnp.concatenate([other, own], axis=axis),
    )


def to_window(cube, z, c):
    held = cross(trade_z(cube, z))
    other = swap(held, "win", 1)
    both = ordered(c == 0, held[:, None], other[:, None], 1)
    return both.reshape(-1, cube.shape[-1])


def from_window(partial, z, c, count, rows):
    cube = partial.reshape(count, 2, rows, partial.shape[-1])
    keep = lax.dynamic_index_in_dim(cube, c, 1, keepdims=False)
    send = lax.dynamic_index_in_dim(cube, 1 - c, 1, keepdims=False).astype(BF)
    held = (keep + swap(send, "win", 1).astype(F32)).astype(BF)
    return trade_z(cross(held), z)


def steps_of(order):
    found = []
    for letter in order:
        if letter == "x":
            found.append(("seq", 0))
        elif letter == "y":
            found += [("win", b) for b in range(1, lax.axis_size("win").bit_length() - 1)]
        else:
            found += [("seq", b) for b in range(1, lax.axis_size("seq").bit_length() - 1)]
    return found


def bit_of(axis, bit):
    return (lax.axis_index(axis) >> bit) & 1


def reduce_rows(terms, steps):
    held = terms
    for axis, bit in steps:
        half = held.shape[0] // 2
        own = bit_of(axis, bit)
        send = lax.dynamic_slice_in_dim(held, (1 - own) * half, half, 0)
        keep = lax.dynamic_slice_in_dim(held, own * half, half, 0)
        held = (keep.astype(F32) + swap(send, axis, 1 << bit).astype(F32)).astype(BF)
    return held


def gather_rows(share, steps):
    held = share
    for axis, bit in reversed(steps):
        held = ordered(bit_of(axis, bit) == 0, held, swap(held, axis, 1 << bit), 0)
    return held


def sum_rows(terms, order):
    steps = steps_of(order)
    return gather_rows(reduce_rows(terms, steps), steps)


def body(
    inputs,
    cotangent,
    offsets,
    end_flags,
    ln_gain,
    ln_bias,
    w_query,
    w_key,
    w_value,
    w_proj,
    w_in,
    b_in,
    w_out,
    b_out,
):
    count, rows, width = inputs.shape
    hidden = w_in.shape[1]
    tokens = count * rows
    n_seq = lax.axis_size("seq")
    assert 2 * count == n_seq
    seq, win = lax.axis_index("seq"), lax.axis_index("win")
    z, x, c = seq // 2, seq % 2, win % 2
    half_d, half_f = width // 2, hidden // 2

    def cols_of(weight, size):
        return lax.dynamic_slice_in_dim(weight, c * size, size, 1)

    def rows_of(weight, size):
        return lax.dynamic_slice_in_dim(weight, c * size, size, 0)

    flat_in = inputs.reshape(tokens, width).astype(F32)
    normed_full, norm_back = jax.vjp(layernorm, flat_in, ln_gain, ln_bias)
    normed = normed_full.astype(BF)
    grad_low = cotangent.reshape(tokens, width)
    grad_full = grad_low.astype(F32)

    bounds = jnp.where(end_flags == 1, offsets, 0).astype(jnp.int32)
    normed_win = to_window(normed.reshape(count, rows, width), z, c)
    grad_win = to_window(cotangent, z, c)

    normed_chip = jnp.concatenate([normed, swap(normed, "win", 1)], axis=0)
    grad_chip = jnp.concatenate([grad_low, swap(grad_low, "win", 1)], axis=0)
    w_in_half, w_out_half = cols_of(w_in, half_f), rows_of(w_out, half_f)
    b_in_half = lax.dynamic_slice_in_dim(b_in, c * half_f, half_f, 0)
    inner = dot(normed_chip, w_in_half) + b_in_half
    act_full, gelu_back = jax.vjp(gelu_tanh, inner)
    act = act_full.astype(BF)
    grad_w_out = dot(act, grad_chip, 0, 0).astype(BF)
    sum_out = sum_rows(grad_w_out, "yxz")
    grad_inner = gelu_back(dot(grad_chip, w_out_half, 1, 1))[0].astype(BF)
    grad_w_in = dot(normed_chip, grad_inner, 0, 0).astype(BF)
    sum_in = sum_rows(grad_w_in, "xyz")
    grad_b_in = jnp.sum(grad_inner.astype(F32), axis=0)
    ff_out = dot(act, w_out_half)
    ff_out = ff_out[:tokens] + swap(ff_out[tokens:].astype(BF), "win", 1).astype(F32)
    ff_back = dot(grad_inner, w_in_half, 1, 1)
    ff_back = ff_back[:tokens] + swap(ff_back[tokens:].astype(BF), "win", 1).astype(F32)

    other = swap(bounds.astype(F32), "win", 1).astype(jnp.int32)
    bound = lax.dynamic_index_in_dim(jnp.where(x == c, bounds, other), z, 0, keepdims=False)
    w_q, w_k, w_v = (cols_of(weight, half_d) for weight in (w_query, w_key, w_value))
    w_p = rows_of(w_proj, half_d)
    turns = tables(n_seq * rows, LANES, HEAD_DIM, ROT, 0)
    mixed, grad_q, grad_k, grad_v = attention(
        bound,
        dot(normed_win, w_q),
        dot(normed_win, w_k),
        dot(normed_win, w_v).astype(BF),
        dot(grad_win, w_p, 1, 1).astype(BF),
        turns,
    )
    grad_heads = jnp.concatenate(
        [dot(normed_win, grad, 0, 0).astype(BF) for grad in (grad_q, grad_k, grad_v)]
        + [dot(grad_win, mixed, 0, 0).astype(BF)],
        axis=1,
    )
    sum_heads = sum_rows(grad_heads, "zyx")
    heads_back = dot(grad_q, w_q, 1, 1) + dot(grad_k, w_k, 1, 1) + dot(grad_v, w_v, 1, 1)
    heads_back = from_window(heads_back, z, c, count, rows)
    heads_out = from_window(dot(mixed, w_p), z, c, count, rows)

    result = flat_in + heads_out.reshape(tokens, width).astype(F32) + ff_out + b_out
    outputs = result.astype(BF).reshape(inputs.shape)
    grad_normed = ff_back + heads_back.reshape(tokens, width).astype(F32)
    grad_flat, grad_ln_gain, grad_ln_bias = norm_back(grad_normed)
    grad_inputs = (grad_full + grad_flat).reshape(inputs.shape)

    small = jnp.concatenate(
        [
            grad_ln_gain,
            grad_ln_bias,
            lax.dynamic_update_slice_in_dim(jnp.zeros_like(b_in), grad_b_in, c * half_f, 0),
            jnp.sum(grad_full, axis=0),
        ]
    )
    small = lax.psum(small, ("seq", "win"))
    sum_ln_gain, sum_ln_bias, sum_b_in, sum_b_out = jnp.split(
        small, [width, 2 * width, 2 * width + hidden]
    )

    sum_w_in = ordered(c == 0, sum_in, swap(sum_in, "win", 1), 1).astype(F32)
    sum_w_out = ordered(c == 0, sum_out, swap(sum_out, "win", 1), 0).astype(F32)
    heads_other = swap(sum_heads, "win", 1)
    sums = [
        ordered(
            c == 0,
            sum_heads[:, i * half_d : (i + 1) * half_d],
            heads_other[:, i * half_d : (i + 1) * half_d],
            1,
        ).astype(F32)
        for i in range(4)
    ]
    return (
        outputs,
        grad_inputs,
        sum_ln_gain,
        sum_ln_bias,
        sums[0],
        sums[1],
        sums[2],
        sums[3].T,
        sum_w_in,
        sum_b_in,
        sum_w_out,
        sum_b_out,
    )


def solution(mesh):
    cube = P("win", "seq", None)
    return jax.shard_map(
        body,
        mesh=mesh,
        in_specs=(cube, cube, P("win"), P("win")) + (P(),) * 10,
        out_specs=(cube, cube) + (P(),) * 10,
        check_vma=False,
    )
```

```python
import functools
import math

import jax
import jax.numpy as jnp
import numpy as np
from jax import lax
from jax.experimental import pallas as pl
from jax.experimental.pallas import tpu as pltpu
from jax.sharding import PartitionSpec as P

HEAD_DIM = 64
ROT = 32
LANES = 128
BF = jnp.bfloat16
F32 = jnp.float32


def tables(count):
    column = np.arange(LANES) % HEAD_DIM
    frequency = np.exp((column // 2) * (-2.0 * math.log(10000.0) / ROT)).astype(np.float32)
    angles = (np.arange(count, dtype=np.float32)[:, None] * frequency).astype(np.float64)
    rotated = column < ROT
    even = column % 2 == 0
    cosine = np.where(rotated, np.cos(angles), 1.0)
    sine = np.where(rotated, np.sin(angles), 0.0)
    ahead = np.where(even, -sine, 0.0)
    behind = np.where(even, 0.0, sine)
    return [jnp.asarray(table, F32) for table in (cosine, ahead, behind)]


def layernorm(values, gain, shift):
    center = values - jnp.mean(values, axis=-1, keepdims=True)
    spread = jnp.mean(center * center, axis=-1, keepdims=True)
    return center * lax.rsqrt(spread + 1e-05) * gain + shift


def norm_kernel(inputs_ref, grad_ref, gain_ref, bias_ref, pair_ref):
    values = inputs_ref[0].astype(F32)
    pair_ref[0, 0] = layernorm(values, gain_ref[...], bias_ref[...]).astype(BF)
    pair_ref[0, 1] = grad_ref[0]


def norm_pair(inputs, cotangent, gain, bias):
    count, rows, width = inputs.shape
    cube = pl.BlockSpec((1, rows, width), lambda i: (i, 0, 0))
    return pl.pallas_call(
        norm_kernel,
        grid=(count,),
        in_specs=[cube, cube, whole((1, width)), whole((1, width))],
        out_specs=pl.BlockSpec((1, 2, rows, width), lambda i: (i, 0, 0, 0)),
        out_shape=jax.ShapeDtypeStruct((count, 2, rows, width), BF),
        cost_estimate=small_cost(),
    )(inputs, cotangent, gain.reshape(1, -1), bias.reshape(1, -1))


def dot(left, right, left_dim=1, right_dim=0):
    return lax.dot_general(
        left, right, (((left_dim,), (right_dim,)), ((), ())), preferred_element_type=F32
    )


def after(values, *gates):
    return lax.optimization_barrier((values, gates))[0]


def small_cost():
    return pl.CostEstimate(flops=1 << 20, bytes_accessed=1 << 16, transcendentals=0)


def whole(shape):
    return pl.BlockSpec(shape, lambda *at: (0,) * len(shape))


def gelu_both(values):
    scale, cubic = math.sqrt(2.0 / math.pi), 0.044715
    square = values * values
    tanh = jnp.tanh(scale * values * (1.0 + cubic * square))
    half = 0.5 * (1.0 + tanh)
    slope = half + 0.5 * scale * values * (1.0 - tanh * tanh) * (1.0 + 3.0 * cubic * square)
    return values * half, slope


def ff_kernel(
    units_ref, own_ref, other_ref, w_in_ref, b_in_ref, w_out_ref,
    first_ref, second_ref, act_ref, inner_ref, bias_ref,
    normed, grad, normed_turned,
):
    step = pl.program_id(0)
    count, _, rows, _ = own_ref.shape

    @pl.when(step == 0)
    def _():
        for place, ref in enumerate((own_ref, other_ref)):
            for i in range(count):
                at = slice((place * count + i) * rows, (place * count + i + 1) * rows)
                normed[at] = ref[i, 0]
                grad[at] = ref[i, 1]
        normed_turned[...] = normed[...].T

    act, slope = gelu_both(dot(normed[...], w_in_ref[...]) + b_in_ref[...])
    act = act.astype(BF)
    act_ref[...] = act
    grad_inner = (dot(grad[...], w_out_ref[...], 1, 1) * slope).astype(BF)
    inner_ref[...] = grad_inner
    bias_ref[...] = jnp.sum(grad_inner.astype(F32), axis=0, keepdims=True)
    units = act.shape[1]
    grad_w_out = dot(act, grad[...], 0, 0).astype(BF)
    grad_w_in = dot(normed_turned[...], grad_inner).astype(BF)

    def store(ref):
        ref[:units] = grad_w_out
        ref[units:, :units] = grad_w_in[:units]
        ref[units:, units:] = grad_w_in[units:]

    pl.when(step == 0)(lambda: store(first_ref))
    pl.when(step == 1)(lambda: store(second_ref))


def feed_forward(units, own, other, w_in, b_in, w_out):
    tokens, width = own.shape[0] * own.shape[2], own.shape[3]
    size = w_in.shape[1] // 8
    block = pl.BlockSpec((2 * tokens, size), lambda step, units: (0, step))
    return pl.pallas_call(
        ff_kernel,
        grid_spec=pltpu.PrefetchScalarGridSpec(
            num_scalar_prefetch=1,
            grid=(2,),
            in_specs=[whole(own.shape)] * 2
            + [
                pl.BlockSpec((width, size), lambda step, units: (0, units[step])),
                pl.BlockSpec((1, size), lambda step, units: (0, units[step])),
                pl.BlockSpec((size, width), lambda step, units: (units[step], 0)),
            ],
            out_specs=[whole((2 * size, width))] * 2
            + [block, block, pl.BlockSpec((1, size), lambda step, units: (0, step))],
            scratch_shapes=[
                pltpu.VMEM((2 * tokens, width), BF),
                pltpu.VMEM((2 * tokens, width), BF),
                pltpu.VMEM((width, 2 * tokens), BF),
            ],
        ),
        out_shape=[jax.ShapeDtypeStruct((2 * size, width), BF)] * 2
        + [jax.ShapeDtypeStruct((2 * tokens, 2 * size), BF)] * 2
        + [jax.ShapeDtypeStruct((1, 2 * size), F32)],
        compiler_params=pltpu.CompilerParams(vmem_limit_bytes=56 << 20),
        cost_estimate=small_cost(),
    )(units, own, other, w_in, b_in, w_out)


def ff_ends_kernel(
    units_ref, act_ref, act_late_ref, inner_ref, inner_late_ref, w_in_ref, w_out_ref,
    kept, sent, out_sum, back_sum,
):
    step = pl.program_id(0)
    tokens = kept.shape[1]

    def terms(act, inner):
        return dot(act[...], w_out_ref[...]), dot(inner[...], w_in_ref[...], 1, 1)

    @pl.when(step == 0)
    def _():
        out_sum[...], back_sum[...] = terms(act_ref, inner_ref)

    @pl.when(step == 1)
    def _():
        out, back = terms(act_ref, inner_ref)
        out_sum[...] += out
        back_sum[...] += back

    @pl.when(step >= 2)
    def _():
        out, back = terms(act_late_ref, inner_late_ref)
        out_sum[...] += out
        back_sum[...] += back

    @pl.when(step == 3)
    def _():
        for i, sums in enumerate((out_sum, back_sum)):
            kept[i] = sums[:tokens]
            sent[i] = sums[tokens:].astype(BF)


def ff_ends(units, act, act_late, inner, inner_late, w_in, w_out):
    tokens2, size2 = act.shape
    width, size, tokens = w_in.shape[0], size2 // 2, tokens2 // 2
    early = pl.BlockSpec((tokens2, size), lambda step, units: (0, jnp.minimum(step, 1)))
    late = pl.BlockSpec((tokens2, size), lambda step, units: (0, jnp.maximum(step - 2, 0)))
    return pl.pallas_call(
        ff_ends_kernel,
        grid_spec=pltpu.PrefetchScalarGridSpec(
            num_scalar_prefetch=1,
            grid=(4,),
            in_specs=[
                early, late, early, late,
                pl.BlockSpec((width, size), lambda step, units: (0, units[step])),
                pl.BlockSpec((size, width), lambda step, units: (units[step], 0)),
            ],
            out_specs=[whole((2, tokens, width))] * 2,
            scratch_shapes=[pltpu.VMEM((tokens2, width), F32)] * 2,
        ),
        out_shape=[
            jax.ShapeDtypeStruct((2, tokens, width), F32),
            jax.ShapeDtypeStruct((2, tokens, width), BF),
        ],
        compiler_params=pltpu.CompilerParams(vmem_limit_bytes=56 << 20),
        cost_estimate=small_cost(),
    )(units, act, act_late, inner, inner_late, w_in, w_out)


def attend(bound, query, key, value, grad, rotate_back, scratch, block):
    k_turned, v_turned, mixed_turned, gq_turned, gk_sum, gv_sum = scratch
    count, lanes = query.shape
    k_turned[...] = key.T
    v_turned[...] = value.T
    gk_sum[...] = jnp.zeros_like(gk_sum)
    gv_sum[...] = jnp.zeros_like(gv_sum)
    lane = lax.broadcasted_iota(jnp.int32, (count, lanes), 1)
    for head in range(lanes // HEAD_DIM):
        cols = slice(head * HEAD_DIM, (head + 1) * HEAD_DIM)
        mine = (lane >= head * HEAD_DIM) & (lane < (head + 1) * HEAD_DIM)
        q_head = jnp.where(mine, query, jnp.zeros_like(query))
        g_head = jnp.where(mine, grad, jnp.zeros_like(grad))
        for start in range(0, count, block):
            seen = start + block
            rows = slice(start, seen)
            scores = dot(key[:seen], q_head[rows], 1, 1)
            at_key = lax.broadcasted_iota(jnp.int32, (seen, block), 0)
            at_query = lax.broadcasted_iota(jnp.int32, (1, block), 1) + start
            lowest = jnp.where(at_query >= bound, bound, 0)
            scores = jnp.where((at_key <= at_query) & (at_key >= lowest), scores, -1e30)
            probs = jnp.exp(scores - jnp.max(scores, axis=0, keepdims=True))
            probs = probs * (1.0 / jnp.sum(probs, axis=0, keepdims=True))
            probs_low = probs.astype(BF)
            grad_probs = dot(value[:seen], g_head[rows], 1, 1)
            row_dot = jnp.sum(probs * grad_probs, axis=0, keepdims=True)
            grad_scores = (probs * (grad_probs - row_dot)).astype(BF)
            mixed_turned[cols, rows] = dot(v_turned[cols, :seen], probs_low)
            gq_turned[cols, rows] = dot(k_turned[cols, :seen], grad_scores)
            gv_sum[:seen, :] += dot(probs_low, g_head[rows])
            gk_sum[:seen, :] += dot(grad_scores, q_head[rows])
    grad_query = (gq_turned[...].T * HEAD_DIM ** -0.5).astype(BF).astype(F32)
    return (
        rotate_back(grad_query).astype(BF),
        rotate_back(gk_sum[...].astype(BF).astype(F32)).astype(BF),
        gv_sum[...].astype(BF),
    )


def heads_kernel(
    scalars_ref, held, there, w_q_ref, w_k_ref, w_v_ref, w_p_ref,
    cos_ref, ahead_ref, behind_ref, *rest, late, block,
):
    if late:
        out_before, back_before, first, second, kept, sent = rest[:6]
    else:
        first, second, out_after, back_after = rest[:4]
    normed_ref, grad_ref, normed_turned, mixed_all, grads_all, proj_all, weights_all = rest[-13:-6]
    scratch = rest[-6:]
    step = pl.program_id(0)
    bound, core = scalars_ref[0], scalars_ref[3]
    count, width = normed_ref.shape
    chunks, _, rows, _ = held.shape

    def at(index):
        return pl.ds(pl.multiple_of(index * rows, rows), rows)

    lanes = w_q_ref.shape[1]
    cosine, ahead, behind = cos_ref[...], ahead_ref[...], behind_ref[...]

    def rotate(values):
        return (
            values * cosine
            + pltpu.roll(values, lanes - 1, 1) * ahead
            + pltpu.roll(values, 1, 1) * behind
        )

    def rotate_back(grads):
        return (
            grads * cosine
            + pltpu.roll(grads * ahead, 1, 1)
            + pltpu.roll(grads * behind, lanes - 1, 1)
        )

    @pl.when(step == 0)
    def _():
        for i in range(chunks):
            mine, other = at(2 * i + core), at(2 * i + 1 - core)
            normed_ref[mine, :] = held[i, 0]
            normed_ref[other, :] = there[i, 0]
            grad_ref[mine, :] = held[i, 1]
            grad_ref[other, :] = there[i, 1]
        normed_turned[...] = normed_ref[...].T

    weights = jnp.concatenate([w_q_ref[...], w_k_ref[...], w_v_ref[...]], axis=1)
    raw = dot(normed_ref[...], weights)
    query = (rotate(raw[:, :lanes]).astype(BF).astype(F32) * HEAD_DIM ** -0.5).astype(BF)
    key = rotate(raw[:, lanes : 2 * lanes]).astype(BF)
    value = raw[:, 2 * lanes :].astype(BF)
    grad_mixed = dot(grad_ref[...], w_p_ref[...], 1, 1).astype(BF)
    parts = attend(bound, query, key, value, grad_mixed, rotate_back, scratch, block)
    mixed_turned = scratch[2][...].astype(BF)
    grads = jnp.concatenate(parts, axis=1)
    grad_weights = dot(normed_turned[...], grads).astype(BF)
    grad_proj = dot(mixed_turned, grad_ref[...]).astype(BF)

    def store(ref):
        ref[:lanes] = grad_proj
        for i in range(3):
            for j in range(width // lanes):
                ref[(i + 1) * lanes : (i + 2) * lanes, j * lanes : (j + 1) * lanes] = grad_weights[
                    j * lanes : (j + 1) * lanes, i * lanes : (i + 1) * lanes
                ]

    def keep(index):
        mixed_all[:, index * lanes : (index + 1) * lanes] = scratch[2][...].T.astype(BF)
        grads_all[:, 3 * index * lanes : 3 * (index + 1) * lanes] = grads
        proj_all[index * lanes : (index + 1) * lanes] = w_p_ref[...]
        weights_all[:, 3 * index * lanes : 3 * (index + 1) * lanes] = weights

    @pl.when(step == 0)
    def _():
        store(first)
        keep(0)

    @pl.when(step == 1)
    def _():
        store(second)
        keep(1)
        out = dot(mixed_all[...], proj_all[...])
        back = dot(grads_all[...], weights_all[...], 1, 1)
        if not late:
            out_after[...] = out
            back_after[...] = back
            return
        out_before[...] += out
        back_before[...] += back
        for i in range(chunks):
            mine, other = at(2 * i + core), at(2 * i + 1 - core)
            for j, sums in enumerate((out_before, back_before)):
                kept[i, j] = sums[mine, :]
                sent[i, j] = sums[other, :].astype(BF)


def attention(scalars, window, w_query, w_key, w_value, w_proj, turns, before=()):
    chunks, _, rows, width = window[0].shape
    count = 2 * chunks * rows
    late = bool(before)
    cols = pl.BlockSpec((width, LANES), lambda step, s: (0, s[1 + step]))
    sums = jax.ShapeDtypeStruct((4 * LANES, width), BF)
    if late:
        shape = window[0].shape
        outs = [jax.ShapeDtypeStruct(shape, F32), jax.ShapeDtypeStruct(shape, BF)]
    else:
        outs = [jax.ShapeDtypeStruct((count, width), F32)] * 2
    return pl.pallas_call(
        functools.partial(heads_kernel, late=late, block=512),
        grid_spec=pltpu.PrefetchScalarGridSpec(
            num_scalar_prefetch=1,
            grid=(2,),
            in_specs=[whole(window[0].shape)] * 2
            + [cols] * 3
            + [pl.BlockSpec((LANES, width), lambda step, s: (s[1 + step], 0))]
            + [whole((count, LANES))] * 3
            + [whole((count, width))] * len(before),
            out_specs=[whole(sums.shape)] * 2 + [whole(out.shape) for out in outs],
            scratch_shapes=[
                pltpu.VMEM((count, width), BF),
                pltpu.VMEM((count, width), BF),
                pltpu.VMEM((width, count), BF),
                pltpu.VMEM((count, 2 * LANES), BF),
                pltpu.VMEM((count, 6 * LANES), BF),
                pltpu.VMEM((2 * LANES, width), BF),
                pltpu.VMEM((width, 6 * LANES), BF),
            ]
            + [pltpu.VMEM((LANES, count), BF)] * 2
            + [pltpu.VMEM((LANES, count), F32)] * 2
            + [pltpu.VMEM((count, LANES), F32)] * 2,
        ),
        out_shape=[sums, sums] + outs,
        compiler_params=pltpu.CompilerParams(vmem_limit_bytes=60 << 20),
        cost_estimate=small_cost(),
    )(scalars, *window, w_query, w_key, w_value, w_proj, *turns, *before)


def place_ff_kernel(out_ref, in_ref, w_out_ref, w_in_ref):
    size = w_in_ref.shape[2]
    w_out_ref[...] = out_ref[0].astype(F32)
    both = in_ref[0].astype(F32)
    w_in_ref[0] = both[:, :size]
    w_in_ref[1] = both[:, size:]


def place_ff(parts, orders):
    devices, rows, width = parts.shape
    rows = rows // 2
    shares = devices // 8

    def split(step):
        return step // (4 * shares), step // (2 * shares) % 2, step // shares % 2, step % shares

    def source(step, of_in):
        core, chain, first, share = split(step)
        index = (first * 2 + of_in) * shares + share
        a_side, b_side = (device_of(core, index, steps) for steps in orders)
        return (jnp.where(chain == 0, a_side, b_side), chain, 0)

    def block_of(step):
        core, chain, first, share = split(step)
        return core * 4 + chain * 2 + first, share

    size = width // 2
    return pl.pallas_call(
        place_ff_kernel,
        grid=(devices,),
        in_specs=[
            pl.BlockSpec((1, rows, width), lambda step: source(step, 0)),
            pl.BlockSpec((1, rows, width), lambda step: source(step, 1)),
        ],
        out_specs=[
            pl.BlockSpec(
                (rows, width), lambda step: (block_of(step)[0] * shares + block_of(step)[1], 0)
            ),
            pl.BlockSpec(
                (2, rows, size), lambda step: (0, block_of(step)[1], block_of(step)[0])
            ),
        ],
        out_shape=[
            jax.ShapeDtypeStruct((devices * rows, width), F32),
            jax.ShapeDtypeStruct((2, shares * rows, 8 * size), F32),
        ],
        compiler_params=pltpu.CompilerParams(vmem_limit_bytes=60 << 20),
        cost_estimate=small_cost(),
    )(parts, parts)


def place_heads_kernel(parts_ref, q_out, k_out, v_out, p_out, *, source):
    pair = pl.program_id(0)
    rows, width = parts_ref.shape[1] // 2, parts_ref.shape[2]
    for share in range(4 * LANES // rows):
        both = parts_ref[source(pair, share)].astype(F32)
        part = jnp.where(pair // 2 % 2 == 0, both[:rows], both[rows:])
        place, start = divmod(share * rows, LANES)
        if place == 0:
            p_out[start : start + rows] = part
            continue
        out = (q_out, k_out, v_out)[place - 1]
        for j in range(width // LANES):
            out[j * LANES + start : j * LANES + start + rows, :] = part[
                :, j * LANES : (j + 1) * LANES
            ]


def device_of(core, index, steps):
    seq, win = 0, core
    for place, (axis, bit) in enumerate(steps):
        value = (index // 2 ** (len(steps) - 1 - place)) % 2 * 2**bit
        seq, win = (seq + value, win) if axis == "seq" else (seq, win + value)
    return seq * lax.axis_size("win") + win


def place_heads(parts, orders):
    devices, rows, width = parts.shape
    shares = devices // 4

    def source(pair, share):
        index = pair % 2 * shares + share
        a_side, b_side = (device_of(pair // 4, index, steps) for steps in orders)
        return jnp.where(pair // 2 % 2 == 0, a_side, b_side)

    cols = pl.BlockSpec((width, LANES), lambda pair: (0, pair))
    return pl.pallas_call(
        functools.partial(place_heads_kernel, source=source),
        grid=(width // LANES,),
        in_specs=[whole(parts.shape)],
        out_specs=[cols] * 3 + [pl.BlockSpec((LANES, width), lambda pair: (pair, 0))],
        out_shape=[jax.ShapeDtypeStruct((width, width), F32)] * 4,
        compiler_params=pltpu.CompilerParams(vmem_limit_bytes=60 << 20),
        cost_estimate=small_cost(),
    )(parts)


def swap(values, axis, bits):
    return lax.ppermute(
        values, axis, [(i, i ^ bits) for i in range(lax.axis_size(axis))]
    )


def cross(values):
    n_seq, n_win = lax.axis_size("seq"), lax.axis_size("win")
    pairs = []
    for s in range(n_seq):
        for w in range(n_win):
            if s % 2 != w % 2:
                s_to, w_to = (s & ~1) | (w & 1), (w & ~1) | (s & 1)
                pairs.append((s * n_win + w, s_to * n_win + w_to))
    return values, lax.ppermute(values, ("seq", "win"), pairs)


def crossed(pair):
    stays = lax.axis_index("seq") % 2 == lax.axis_index("win") % 2
    return jnp.where(stays, *pair)


def trade_z(cubes, z):
    def entry(k):
        at = [lax.dynamic_index_in_dim(cube, z ^ k, 0, keepdims=True) for cube in cubes]
        return crossed(at)

    count = cubes[0].shape[0]
    return [entry(0)] + [swap(entry(k), "seq", 2 * k) for k in range(1, count)]


def land_kernel(z_ref, *refs):
    for k in range(len(refs) - 1):

        @pl.when(pl.program_id(0) == k)
        def _():
            refs[-1][...] = refs[k][...]


def landed(entries, z):
    count = len(entries)
    shape = entries[0].shape
    return pl.pallas_call(
        land_kernel,
        grid_spec=pltpu.PrefetchScalarGridSpec(
            num_scalar_prefetch=1,
            grid=(count,),
            in_specs=[whole(shape)] * count,
            out_specs=pl.BlockSpec(shape, lambda k, z: (z[0] ^ k, 0, 0, 0)),
        ),
        out_shape=jax.ShapeDtypeStruct((count,) + shape[1:], BF),
        cost_estimate=small_cost(),
    )(z.reshape(1), *entries)


def ordered(first_is_own, own, other, axis):
    return jnp.where(
        first_is_own,
        jnp.concatenate([own, other], axis=axis),
        jnp.concatenate([other, own], axis=axis),
    )


def steps_of(order):
    n_seq, n_win = lax.axis_size("seq"), lax.axis_size("win")
    found = []
    for letter in order:
        if letter == "x":
            bits = [("seq", 0)]
        elif letter == "y":
            bits = [("win", b) for b in range(1, n_win.bit_length() - 1)]
        else:
            bits = [("seq", b) for b in range(1, n_seq.bit_length() - 1)]
        found += bits[::-1] if letter == "Z" else bits
    return found


def bit_of(step):
    axis, bit = step
    return (lax.axis_index(axis) >> bit) & 1


def trade(values, step):
    axis, bit = step
    return swap(values, axis, 1 << bit)


def reduce_step(terms, step):
    half = terms[-1][0].shape[0] // 2
    own = bit_of(step)
    sent = rows_sum([(array, at + (1 - own) * half) for array, at in terms], half)
    return [(array, at + own * half) for array, at in terms] + [(trade(sent, step), 0)], sent


def rows_sum(terms, rows):
    parts = [lax.dynamic_slice_in_dim(array, at, rows, 0) for array, at in terms]
    return sum(part.astype(F32) for part in parts).astype(BF)


def summed(terms):
    return rows_sum(terms, terms[-1][0].shape[0])


def gather_step(share, step):
    return ordered(bit_of(step) == 0, share, trade(share, step), 0)


def body(
    inputs,
    cotangent,
    offsets,
    end_flags,
    ln_gain,
    ln_bias,
    w_query,
    w_key,
    w_value,
    w_proj,
    w_in,
    b_in,
    w_out,
    b_out,
):
    count, rows, width = inputs.shape
    hidden = w_in.shape[1]
    tokens = count * rows
    n_seq = lax.axis_size("seq")
    assert 2 * count == n_seq
    seq, win = lax.axis_index("seq"), lax.axis_index("win")
    z, x, y, c = seq // 2, seq % 2, win // 2 % 2, win % 2
    first_a, first_b = steps_of("x"), steps_of("y")[:1]
    rest_a, rest_b = steps_of("yz"), steps_of("y")[1:] + steps_of("xZ")
    own_a, own_b = bit_of(first_a[0]), bit_of(first_b[0])
    core = c * 4
    sent = jnp.stack([core + 1 - own_a, core + 3 - own_b]).astype(jnp.int32)
    kept = jnp.stack([core + own_a, core + 2 + own_b]).astype(jnp.int32)

    bounds = jnp.where(end_flags == 1, offsets, 0).astype(F32)
    bounds = jnp.where(x == c, bounds, swap(bounds, "win", 1)).astype(jnp.int32)
    bound = lax.dynamic_index_in_dim(bounds, z, 0, keepdims=False)
    turns = tables(n_seq * rows)

    pair = norm_pair(inputs, cotangent, ln_gain, ln_bias)
    pair_other = swap(pair, "win", 1)
    pair_cross = cross(pair)

    ff_args = (pair, pair_other, w_in, b_in.reshape(1, -1), w_out)
    a_sent, b_sent, act, inner, bias = feed_forward(sent, *ff_args)
    a_got, b_got = trade(a_sent, first_a[0]), trade(b_sent, first_b[0])
    entries = trade_z(after(pair_cross, bias), z)
    a_kept, b_kept, act_late, inner_late, bias_late = feed_forward(
        after(kept, bias, entries[0]), *ff_args
    )
    ff_kept, ff_sent = ff_ends(
        after(jnp.concatenate([sent, kept]), bias_late), act, act_late, inner, inner_late, w_in, w_out
    )

    ff_other = swap(ff_sent, "win", 1)
    a_got, b_got = after((a_got, b_got), ff_kept)
    a_terms, a_went = reduce_step([(a_kept, 0), (a_got, 0)], rest_a[0])
    b_terms, b_went = reduce_step([(b_kept, 0), (b_got, 0)], rest_b[0])
    held = landed(after(entries, a_went, b_went), z)
    there = swap(held, "win", 1)
    attn_args = ((held, there), w_query, w_key, w_value, w_proj, turns)
    head = jnp.stack([bound])
    ha_sent, hb_sent, heads_out, heads_back = attention(
        jnp.concatenate([head, sent, c.reshape(1)]), *attn_args
    )
    a_terms, b_terms, ha_sent, hb_sent = after((a_terms, b_terms, ha_sent, hb_sent), heads_out)
    (a_terms, a_went), (b_terms, b_went) = reduce_step(a_terms, rest_a[1]), reduce_step(b_terms, rest_b[1])
    ha_got, hb_got = trade(ha_sent, first_a[0]), trade(hb_sent, first_b[0])
    ha_kept, hb_kept, heads_kept, heads_sent = attention(
        after(jnp.concatenate([head, kept, c.reshape(1)]), a_went, b_went, ff_other),
        *attn_args,
        before=(heads_out, heads_back),
    )

    ha_terms, hb_terms = [(ha_kept, 0), (ha_got, 0)], [(hb_kept, 0), (hb_got, 0)]
    a_terms, b_terms, ha_terms, hb_terms, heads_sent = after(
        (a_terms, b_terms, ha_terms, hb_terms, heads_sent), heads_kept
    )
    (a_terms, a_went), (b_terms, b_went) = reduce_step(a_terms, rest_a[2]), reduce_step(b_terms, rest_b[2])
    ha_terms, hb_terms = after((ha_terms, hb_terms), a_went, b_went)
    (ha_terms, _), (hb_terms, _) = reduce_step(ha_terms, rest_a[0]), reduce_step(hb_terms, rest_b[0])
    heads_other = swap(heads_sent, "win", 1)
    a_terms, b_terms, ha_terms, hb_terms, heads_other = after(
        (a_terms, b_terms, ha_terms, hb_terms, heads_other)
    )
    for step_a, step_b in zip(rest_a[3:], rest_b[3:]):
        (a_terms, _), (b_terms, _) = reduce_step(a_terms, step_a), reduce_step(b_terms, step_b)
    share = jnp.concatenate([summed(a_terms), summed(b_terms)], axis=0)
    ff_parts = lax.all_gather(share, ("seq", "win"), axis=0, tiled=False)
    ha_terms, hb_terms, heads_other = after((ha_terms, hb_terms, heads_other), share)
    (ha_terms, _), (hb_terms, _) = reduce_step(ha_terms, rest_a[1]), reduce_step(hb_terms, rest_b[1])
    heads_cross = cross((heads_kept + heads_other.astype(F32)).astype(BF))
    ha_terms, hb_terms, heads_cross = after((ha_terms, hb_terms, heads_cross))
    for step_a, step_b in zip(rest_a[2:], rest_b[2:]):
        (ha_terms, _), (hb_terms, _) = reduce_step(ha_terms, step_a), reduce_step(hb_terms, step_b)
    entries = trade_z(heads_cross, z)
    ha_terms, hb_terms = after((ha_terms, hb_terms))
    heads_share = jnp.concatenate([summed(ha_terms), summed(hb_terms)], axis=0)
    heads = landed(after(entries, heads_share), z).astype(F32)
    ff_parts = after(ff_parts, heads)
    heads_parts = lax.all_gather(after(heads_share, ff_parts), ("seq", "win"), axis=0, tiled=False)

    ff = (ff_kept + ff_other.astype(F32)).reshape(2, count, rows, width)
    full_in, grad_full = inputs.astype(F32), cotangent.astype(F32)
    outputs = (full_in + heads[:, 0] + ff[0] + b_out).astype(BF)
    _, norm_back = jax.vjp(layernorm, full_in, ln_gain, ln_bias)
    grad_flat, grad_ln_gain, grad_ln_bias = norm_back(ff[1] + heads[:, 1])
    grad_inputs = grad_full + grad_flat

    grad_b_in = jnp.zeros((8, hidden // 8), F32)
    for units, sums in ((sent, bias), (kept, bias_late)):
        for i in range(2):
            part = sums[:, i * hidden // 8 : (i + 1) * hidden // 8]
            grad_b_in = lax.dynamic_update_slice_in_dim(grad_b_in, part, units[i], 0)
    small = jnp.concatenate(
        [grad_ln_gain, grad_ln_bias, grad_b_in.reshape(-1), jnp.sum(grad_full, axis=(0, 1))]
    ).reshape(-1, LANES)
    for step in first_a + rest_a:
        small = small + trade(small, step)
    small = (small + swap(small, "win", 1)).reshape(-1)
    orders = (first_a + rest_a, first_b + rest_b)
    sum_w_out, sum_w_in = place_ff(ff_parts, orders)
    sum_query, sum_key, sum_value, sum_proj = place_heads(heads_parts, orders)
    sum_ln_gain, sum_ln_bias, sum_b_in, sum_b_out = jnp.split(
        small, [width, 2 * width, 2 * width + hidden]
    )
    return (
        outputs,
        grad_inputs,
        sum_ln_gain,
        sum_ln_bias,
        sum_query,
        sum_key,
        sum_value,
        sum_proj,
        sum_w_in.reshape(width, hidden),
        sum_b_in,
        sum_w_out,
        sum_b_out,
    )


def solution(mesh):
    cube = P("win", "seq", None)
    return jax.shard_map(
        body,
        mesh=mesh,
        in_specs=(cube, cube, P("win"), P("win")) + (P(),) * 10,
        out_specs=(cube, cube) + (P(),) * 10,
        check_vma=False,
    )
```

```python
import functools
import math

import jax
import jax.numpy as jnp
import numpy as np
from jax import lax
from jax.experimental import pallas as pl
from jax.experimental.pallas import tpu as pltpu
from jax.sharding import PartitionSpec as P

HEAD_DIM = 64
ROT = 32
LANES = 128
BF = jnp.bfloat16
F32 = jnp.float32


def tables(count):
    column = np.arange(LANES) % HEAD_DIM
    frequency = np.exp((column // 2) * (-2.0 * math.log(10000.0) / ROT)).astype(np.float32)
    angles = (np.arange(count, dtype=np.float32)[:, None] * frequency).astype(np.float64)
    rotated = column < ROT
    even = column % 2 == 0
    cosine = np.where(rotated, np.cos(angles), 1.0)
    sine = np.where(rotated, np.sin(angles), 0.0)
    ahead = np.where(even, -sine, 0.0)
    behind = np.where(even, 0.0, sine)
    return [jnp.asarray(table, F32) for table in (cosine, ahead, behind)]


def layernorm(values, gain, shift):
    center = values - jnp.mean(values, axis=-1, keepdims=True)
    spread = jnp.mean(center * center, axis=-1, keepdims=True)
    return center * lax.rsqrt(spread + 1e-05) * gain + shift


def norm_kernel(inputs_ref, grad_ref, gain_ref, bias_ref, pair_ref):
    values = inputs_ref[0].astype(F32)
    pair_ref[0, 0] = layernorm(values, gain_ref[...], bias_ref[...]).astype(BF)
    pair_ref[0, 1] = grad_ref[0]


def norm_pair(inputs, cotangent, gain, bias):
    count, rows, width = inputs.shape
    cube = pl.BlockSpec((1, rows, width), lambda i: (i, 0, 0))
    return pl.pallas_call(
        norm_kernel,
        grid=(count,),
        in_specs=[cube, cube, whole((1, width)), whole((1, width))],
        out_specs=pl.BlockSpec((1, 2, rows, width), lambda i: (i, 0, 0, 0)),
        out_shape=jax.ShapeDtypeStruct((count, 2, rows, width), BF),
        cost_estimate=small_cost(),
    )(inputs, cotangent, gain.reshape(1, -1), bias.reshape(1, -1))


def dot(left, right, left_dim=1, right_dim=0):
    return lax.dot_general(
        left, right, (((left_dim,), (right_dim,)), ((), ())), preferred_element_type=F32
    )


def after(values, *gates):
    return lax.optimization_barrier((values, gates))[0]


def small_cost():
    return pl.CostEstimate(flops=1 << 20, bytes_accessed=1 << 16, transcendentals=0)


def whole(shape):
    return pl.BlockSpec(shape, lambda *at: (0,) * len(shape))


def gelu_both(values):
    scale, cubic = math.sqrt(2.0 / math.pi), 0.044715
    square = values * values
    tanh = jnp.tanh(scale * values * (1.0 + cubic * square))
    half = 0.5 * (1.0 + tanh)
    slope = half + 0.5 * scale * values * (1.0 - tanh * tanh) * (1.0 + 3.0 * cubic * square)
    return values * half, slope


def ff_kernel(
    units_ref, own_ref, other_ref, w_in_ref, b_in_ref, w_out_ref,
    first_ref, second_ref, act_ref, inner_ref, bias_ref,
    normed, grad, normed_turned,
):
    step = pl.program_id(0)
    count, _, rows, _ = own_ref.shape

    @pl.when(step == 0)
    def _():
        for place, ref in enumerate((own_ref, other_ref)):
            for i in range(count):
                at = slice((place * count + i) * rows, (place * count + i + 1) * rows)
                normed[at] = ref[i, 0]
                grad[at] = ref[i, 1]
        normed_turned[...] = normed[...].T

    act, slope = gelu_both(dot(normed[...], w_in_ref[...]) + b_in_ref[...])
    act = act.astype(BF)
    act_ref[...] = act
    grad_inner = (dot(grad[...], w_out_ref[...], 1, 1) * slope).astype(BF)
    inner_ref[...] = grad_inner
    bias_ref[...] = jnp.sum(grad_inner.astype(F32), axis=0, keepdims=True)
    units = act.shape[1]
    grad_w_out = dot(act, grad[...], 0, 0).astype(BF)
    grad_w_in = dot(normed_turned[...], grad_inner).astype(BF)

    def store(ref):
        ref[:units] = grad_w_out
        ref[units:, :units] = grad_w_in[:units]
        ref[units:, units:] = grad_w_in[units:]

    pl.when(step == 0)(lambda: store(first_ref))
    pl.when(step == 1)(lambda: store(second_ref))


def feed_forward(units, own, other, w_in, b_in, w_out):
    tokens, width = own.shape[0] * own.shape[2], own.shape[3]
    size = w_in.shape[1] // 8
    block = pl.BlockSpec((2 * tokens, size), lambda step, units: (0, step))
    return pl.pallas_call(
        ff_kernel,
        grid_spec=pltpu.PrefetchScalarGridSpec(
            num_scalar_prefetch=1,
            grid=(2,),
            in_specs=[whole(own.shape)] * 2
            + [
                pl.BlockSpec((width, size), lambda step, units: (0, units[step])),
                pl.BlockSpec((1, size), lambda step, units: (0, units[step])),
                pl.BlockSpec((size, width), lambda step, units: (units[step], 0)),
            ],
            out_specs=[whole((2 * size, width))] * 2
            + [block, block, pl.BlockSpec((1, size), lambda step, units: (0, step))],
            scratch_shapes=[
                pltpu.VMEM((2 * tokens, width), BF),
                pltpu.VMEM((2 * tokens, width), BF),
                pltpu.VMEM((width, 2 * tokens), BF),
            ],
        ),
        out_shape=[jax.ShapeDtypeStruct((2 * size, width), BF)] * 2
        + [jax.ShapeDtypeStruct((2 * tokens, 2 * size), BF)] * 2
        + [jax.ShapeDtypeStruct((1, 2 * size), F32)],
        compiler_params=pltpu.CompilerParams(vmem_limit_bytes=56 << 20),
        cost_estimate=small_cost(),
    )(units, own, other, w_in, b_in, w_out)


def ff_ends_kernel(
    units_ref, act_ref, act_late_ref, inner_ref, inner_late_ref, w_in_ref, w_out_ref,
    kept, sent, out_sum, back_sum,
):
    step = pl.program_id(0)
    tokens = kept.shape[1]

    def terms(act, inner):
        return dot(act[...], w_out_ref[...]), dot(inner[...], w_in_ref[...], 1, 1)

    @pl.when(step == 0)
    def _():
        out_sum[...], back_sum[...] = terms(act_ref, inner_ref)

    @pl.when(step == 1)
    def _():
        out, back = terms(act_ref, inner_ref)
        out_sum[...] += out
        back_sum[...] += back

    @pl.when(step >= 2)
    def _():
        out, back = terms(act_late_ref, inner_late_ref)
        out_sum[...] += out
        back_sum[...] += back

    @pl.when(step == 3)
    def _():
        for i, sums in enumerate((out_sum, back_sum)):
            kept[i] = sums[:tokens]
            sent[i] = sums[tokens:].astype(BF)


def ff_ends(units, act, act_late, inner, inner_late, w_in, w_out):
    tokens2, size2 = act.shape
    width, size, tokens = w_in.shape[0], size2 // 2, tokens2 // 2
    early = pl.BlockSpec((tokens2, size), lambda step, units: (0, jnp.minimum(step, 1)))
    late = pl.BlockSpec((tokens2, size), lambda step, units: (0, jnp.maximum(step - 2, 0)))
    return pl.pallas_call(
        ff_ends_kernel,
        grid_spec=pltpu.PrefetchScalarGridSpec(
            num_scalar_prefetch=1,
            grid=(4,),
            in_specs=[
                early, late, early, late,
                pl.BlockSpec((width, size), lambda step, units: (0, units[step])),
                pl.BlockSpec((size, width), lambda step, units: (units[step], 0)),
            ],
            out_specs=[whole((2, tokens, width))] * 2,
            scratch_shapes=[pltpu.VMEM((tokens2, width), F32)] * 2,
        ),
        out_shape=[
            jax.ShapeDtypeStruct((2, tokens, width), F32),
            jax.ShapeDtypeStruct((2, tokens, width), BF),
        ],
        compiler_params=pltpu.CompilerParams(vmem_limit_bytes=56 << 20),
        cost_estimate=small_cost(),
    )(units, act, act_late, inner, inner_late, w_in, w_out)


def attend(bound, query, key, value, grad, rotate_back, scratch, block):
    k_turned, v_turned, mixed_turned, gq_turned, gk_sum, gv_sum = scratch
    count, lanes = query.shape
    k_turned[...] = key.T
    v_turned[...] = value.T
    gk_sum[...] = jnp.zeros_like(gk_sum)
    gv_sum[...] = jnp.zeros_like(gv_sum)
    lane = lax.broadcasted_iota(jnp.int32, (count, lanes), 1)
    for head in range(lanes // HEAD_DIM):
        cols = slice(head * HEAD_DIM, (head + 1) * HEAD_DIM)
        mine = (lane >= head * HEAD_DIM) & (lane < (head + 1) * HEAD_DIM)
        q_head = jnp.where(mine, query, jnp.zeros_like(query))
        g_head = jnp.where(mine, grad, jnp.zeros_like(grad))
        for start in range(0, count, block):
            seen = start + block
            rows = slice(start, seen)
            scores = dot(key[:seen], q_head[rows], 1, 1)
            at_key = lax.broadcasted_iota(jnp.int32, (seen, block), 0)
            at_query = lax.broadcasted_iota(jnp.int32, (1, block), 1) + start
            lowest = jnp.where(at_query >= bound, bound, 0)
            scores = jnp.where((at_key <= at_query) & (at_key >= lowest), scores, -1e30)
            probs = jnp.exp(scores - jnp.max(scores, axis=0, keepdims=True))
            probs = probs * (1.0 / jnp.sum(probs, axis=0, keepdims=True))
            probs_low = probs.astype(BF)
            grad_probs = dot(value[:seen], g_head[rows], 1, 1)
            row_dot = jnp.sum(probs * grad_probs, axis=0, keepdims=True)
            grad_scores = (probs * (grad_probs - row_dot)).astype(BF)
            mixed_turned[cols, rows] = dot(v_turned[cols, :seen], probs_low)
            gq_turned[cols, rows] = dot(k_turned[cols, :seen], grad_scores)
            gv_sum[:seen, :] += dot(probs_low, g_head[rows])
            gk_sum[:seen, :] += dot(grad_scores, q_head[rows])
    grad_query = (gq_turned[...].T * HEAD_DIM ** -0.5).astype(BF).astype(F32)
    return (
        rotate_back(grad_query).astype(BF),
        rotate_back(gk_sum[...].astype(BF).astype(F32)).astype(BF),
        gv_sum[...].astype(BF),
    )


def heads_kernel(
    scalars_ref, held, there, w_q_ref, w_k_ref, w_v_ref, w_p_ref, cos_ref, ahead_ref, behind_ref,
    mixed_ref, grads_ref, *rest, pairs, block,
):
    sums, (normed_ref, grad_ref, normed_turned), scratch = (
        rest[:pairs], rest[pairs : pairs + 3], rest[pairs + 3 :]
    )
    step = pl.program_id(0)
    bound, core = scalars_ref[0], scalars_ref[1]
    count, width = normed_ref.shape
    chunks, _, rows, _ = held.shape
    lanes = w_q_ref.shape[1]
    cosine, ahead, behind = cos_ref[...], ahead_ref[...], behind_ref[...]

    def at(index):
        return pl.ds(pl.multiple_of(index * rows, rows), rows)

    def rotate(values):
        return (
            values * cosine
            + pltpu.roll(values, lanes - 1, 1) * ahead
            + pltpu.roll(values, 1, 1) * behind
        )

    def rotate_back(grads):
        return (
            grads * cosine
            + pltpu.roll(grads * ahead, 1, 1)
            + pltpu.roll(grads * behind, lanes - 1, 1)
        )

    @pl.when(step == 0)
    def _():
        for i in range(chunks):
            mine, other = at(2 * i + core), at(2 * i + 1 - core)
            normed_ref[mine, :] = held[i, 0]
            normed_ref[other, :] = there[i, 0]
            grad_ref[mine, :] = held[i, 1]
            grad_ref[other, :] = there[i, 1]
        normed_turned[...] = normed_ref[...].T

    weights = jnp.concatenate([w_q_ref[...], w_k_ref[...], w_v_ref[...]], axis=1)
    raw = dot(normed_ref[...], weights)
    query = (rotate(raw[:, :lanes]).astype(BF).astype(F32) * HEAD_DIM ** -0.5).astype(BF)
    key = rotate(raw[:, lanes : 2 * lanes]).astype(BF)
    value = raw[:, 2 * lanes :].astype(BF)
    grad_mixed = dot(grad_ref[...], w_p_ref[...], 1, 1).astype(BF)
    parts = attend(bound, query, key, value, grad_mixed, rotate_back, scratch, block)
    mixed_turned = scratch[2][...].astype(BF)
    mixed_ref[...] = mixed_turned.T
    grads = jnp.concatenate(parts, axis=1)
    grads_ref[...] = grads
    grad_weights = dot(normed_turned[...], grads).astype(BF)
    grad_proj = dot(mixed_turned, grad_ref[...]).astype(BF)

    def store(ref):
        ref[:lanes] = grad_proj
        for i in range(3):
            for j in range(width // lanes):
                ref[(i + 1) * lanes : (i + 2) * lanes, j * lanes : (j + 1) * lanes] = grad_weights[
                    j * lanes : (j + 1) * lanes, i * lanes : (i + 1) * lanes
                ]

    for i in range(pairs):
        pl.when(step == i)(functools.partial(store, sums[i]))


def attention(scalars, pairs, window, w_query, w_key, w_value, w_proj, turns):
    chunks, _, rows, width = window[0].shape
    count = 2 * chunks * rows
    cols = pl.BlockSpec((width, LANES), lambda step, s: (0, s[2 + step]))
    sums = jax.ShapeDtypeStruct((4 * LANES, width), BF)
    return pl.pallas_call(
        functools.partial(heads_kernel, pairs=pairs, block=512),
        grid_spec=pltpu.PrefetchScalarGridSpec(
            num_scalar_prefetch=1,
            grid=(pairs,),
            in_specs=[whole(window[0].shape)] * 2
            + [cols] * 3
            + [pl.BlockSpec((LANES, width), lambda step, s: (s[2 + step], 0))]
            + [whole((count, LANES))] * 3,
            out_specs=[
                pl.BlockSpec((count, LANES), lambda step, s: (0, step)),
                pl.BlockSpec((count, 3 * LANES), lambda step, s: (0, step)),
            ]
            + [whole(sums.shape)] * pairs,
            scratch_shapes=[
                pltpu.VMEM((count, width), BF),
                pltpu.VMEM((count, width), BF),
                pltpu.VMEM((width, count), BF),
            ]
            + [pltpu.VMEM((LANES, count), BF)] * 2
            + [pltpu.VMEM((LANES, count), F32)] * 2
            + [pltpu.VMEM((count, LANES), F32)] * 2,
        ),
        out_shape=[
            jax.ShapeDtypeStruct((count, pairs * LANES), BF),
            jax.ShapeDtypeStruct((count, 3 * pairs * LANES), BF),
        ]
        + [sums] * pairs,
        compiler_params=pltpu.CompilerParams(vmem_limit_bytes=60 << 20),
        cost_estimate=small_cost(),
    )(scalars, *window, w_query, w_key, w_value, w_proj, *turns)


def heads_ends_kernel(
    scalars_ref, *refs, calls,
):
    tensors, (w_q, w_k, w_v, w_p, kept, sent, out_sum, back_sum) = refs[: 2 * calls], refs[2 * calls :]
    step = pl.program_id(0)
    core = scalars_ref[0]
    chunks, _, rows, _ = kept.shape
    first = 0
    for call in range(calls):
        mixed, grads = tensors[2 * call : 2 * call + 2]
        for i in range(mixed.shape[1] // LANES):

            @pl.when(step == first + i)
            def _():
                weights = jnp.concatenate([w_q[...], w_k[...], w_v[...]], axis=1)
                out = dot(mixed[:, i * LANES : (i + 1) * LANES], w_p[...])
                back = dot(grads[:, 3 * i * LANES : 3 * (i + 1) * LANES], weights, 1, 1)
                if first + i == 0:
                    out_sum[...] = out
                    back_sum[...] = back
                else:
                    out_sum[...] += out
                    back_sum[...] += back

        first += mixed.shape[1] // LANES

    @pl.when(step == first - 1)
    def _():
        for i in range(chunks):
            for j, sums in enumerate((out_sum, back_sum)):
                mine = pl.ds(pl.multiple_of((2 * i + core) * rows, rows), rows)
                other = pl.ds(pl.multiple_of((2 * i + 1 - core) * rows, rows), rows)
                kept[i, j] = sums[mine, :]
                sent[i, j] = sums[other, :].astype(BF)


def heads_ends(scalars, parts, shape, w_query, w_key, w_value, w_proj):
    count, width = parts[0][0].shape[0], w_query.shape[0]
    pairs = sum(mixed.shape[1] for mixed, _ in parts) // LANES
    tensors = [tensor for part in parts for tensor in part]
    cols = pl.BlockSpec((width, LANES), lambda step, s: (0, s[1 + step]))
    return pl.pallas_call(
        functools.partial(heads_ends_kernel, calls=len(parts)),
        grid_spec=pltpu.PrefetchScalarGridSpec(
            num_scalar_prefetch=1,
            grid=(pairs,),
            in_specs=[whole(tensor.shape) for tensor in tensors]
            + [cols] * 3
            + [pl.BlockSpec((LANES, width), lambda step, s: (s[1 + step], 0))],
            out_specs=[whole(shape)] * 2,
            scratch_shapes=[pltpu.VMEM((count, width), F32)] * 2,
        ),
        out_shape=[jax.ShapeDtypeStruct(shape, F32), jax.ShapeDtypeStruct(shape, BF)],
        compiler_params=pltpu.CompilerParams(vmem_limit_bytes=60 << 20),
        cost_estimate=small_cost(),
    )(scalars, *tensors, w_query, w_key, w_value, w_proj)


def place_ff_kernel(out_ref, in_ref, w_out_ref, w_in_ref):
    size = w_in_ref.shape[2]
    w_out_ref[...] = out_ref[0].astype(F32)
    both = in_ref[0].astype(F32)
    w_in_ref[0] = both[:, :size]
    w_in_ref[1] = both[:, size:]


def device_of(core, index, steps):
    at = {"x": 0, "y": 0}
    for place, (axis, bit) in enumerate(steps):
        at[axis] = at[axis] + (index // 2 ** (len(steps) - 1 - place)) % 2 * 2**bit
    return (at["x"] * lax.axis_size("y") + at["y"]) * 2 + core


def place_ff(parts, orders):
    devices, held, width = parts.shape
    held, size = held // 2, width // 2
    rows = min(size, held)
    chunks = size // rows

    def split(step):
        return step // (4 * chunks), step // (2 * chunks) % 2, step // chunks % 2, step % chunks

    def source(step, of_in):
        core, chain, first, chunk = split(step)
        row = of_in * size + chunk * rows
        index = first * (width // held) + row // held
        a_side, b_side = (device_of(core, index, steps) for steps in orders)
        return (jnp.where(chain == 0, a_side, b_side), (chain * held + row % held) // rows, 0)

    def block_of(step):
        core, chain, first, chunk = split(step)
        return core * 4 + chain * 2 + first, chunk

    return pl.pallas_call(
        place_ff_kernel,
        grid=(8 * chunks,),
        in_specs=[
            pl.BlockSpec((1, rows, width), lambda step: source(step, 0)),
            pl.BlockSpec((1, rows, width), lambda step: source(step, 1)),
        ],
        out_specs=[
            pl.BlockSpec(
                (rows, width), lambda step: (block_of(step)[0] * chunks + block_of(step)[1], 0)
            ),
            pl.BlockSpec((2, rows, size), lambda step: (0, block_of(step)[1], block_of(step)[0])),
        ],
        out_shape=[
            jax.ShapeDtypeStruct((8 * size, width), F32),
            jax.ShapeDtypeStruct((2, size, 8 * size), F32),
        ],
        compiler_params=pltpu.CompilerParams(vmem_limit_bytes=60 << 20),
        cost_estimate=small_cost(),
    )(parts, parts)


def place_heads_kernel(pairs_ref, a_ref, b_ref, c_ref, d_ref, *rest):
    q_out, k_out, v_out, p_out = rest[-4:]
    lanes, width = p_out.shape
    for index, ref in enumerate((a_ref, b_ref, c_ref, d_ref)):

        @pl.when(pl.program_id(0) == index)
        def _():
            p_out[...] = ref[:lanes].astype(F32)
            for i, out in enumerate((q_out, k_out, v_out)):
                for j in range(width // lanes):
                    out[j * lanes : (j + 1) * lanes, :] = ref[
                        (i + 1) * lanes : (i + 2) * lanes, j * lanes : (j + 1) * lanes
                    ].astype(F32)


def place_heads(pairs, sums, filled=()):
    width = sums[0].shape[1]
    cols = pl.BlockSpec((width, LANES), lambda step, pairs: (0, pairs[step]))
    return pl.pallas_call(
        place_heads_kernel,
        grid_spec=pltpu.PrefetchScalarGridSpec(
            num_scalar_prefetch=1,
            grid=(4,),
            in_specs=[whole(sums[0].shape)] * 4
            + [pl.BlockSpec(memory_space=pl.ANY)] * len(filled),
            out_specs=[cols] * 3
            + [pl.BlockSpec((LANES, width), lambda step, pairs: (pairs[step], 0))],
        ),
        out_shape=[jax.ShapeDtypeStruct((width, width), F32)] * 4,
        input_output_aliases={5 + i: i for i in range(len(filled))},
        compiler_params=pltpu.CompilerParams(vmem_limit_bytes=60 << 20),
        cost_estimate=small_cost(),
    )(pairs, *sums, *filled)


def swap(values, axis, bits):
    return lax.ppermute(
        values, axis, [(i, i ^ bits) for i in range(lax.axis_size(axis))]
    )


def cross(values):
    return values, lax.ppermute(values, ("x", "core"), [(1, 2), (2, 1)])


def crossed(pair):
    return jnp.where(lax.axis_index("x") == lax.axis_index("core"), *pair)


def trade_z(cubes):
    return lax.all_to_all(crossed(cubes), "z", split_axis=0, concat_axis=0, tiled=True)


def trade_parts(cubes, z):
    def entry(k):
        at = [lax.dynamic_index_in_dim(cube, z ^ k, 0, keepdims=True) for cube in cubes]
        return crossed(at)

    count = cubes[0].shape[0]
    return [entry(0)] + [swap(entry(k), "z", k) for k in range(1, count)]


def land_kernel(z_ref, *refs):
    for k in range(len(refs) - 1):

        @pl.when(pl.program_id(0) == k)
        def _():
            refs[-1][...] = refs[k][...]


def landed(entries, z):
    count = len(entries)
    shape = entries[0].shape
    return pl.pallas_call(
        land_kernel,
        grid_spec=pltpu.PrefetchScalarGridSpec(
            num_scalar_prefetch=1,
            grid=(count,),
            in_specs=[whole(shape)] * count,
            out_specs=pl.BlockSpec(shape, lambda k, z: (z[0] ^ k, 0, 0, 0)),
        ),
        out_shape=jax.ShapeDtypeStruct((count,) + shape[1:], BF),
        cost_estimate=small_cost(),
    )(z.reshape(1), *entries)


def ordered(first_is_own, own, other, axis):
    return jnp.where(
        first_is_own,
        jnp.concatenate([own, other], axis=axis),
        jnp.concatenate([other, own], axis=axis),
    )


def steps_of(order):
    found = []
    for letter in order:
        bits = [(letter.lower(), b) for b in range(lax.axis_size(letter.lower()).bit_length() - 1)]
        found += bits[::-1] if letter == "Z" else bits
    return found


def bit_of(step):
    axis, bit = step
    return (lax.axis_index(axis) >> bit) & 1


def trade(values, step):
    axis, bit = step
    return swap(values, axis, 1 << bit)


def sum_kernel(at_ref, *refs, counts):
    first = 0
    for count, out in zip(counts, refs[sum(counts) :]):
        out[...] = sum(ref[...].astype(F32) for ref in refs[first : first + count]).astype(BF)
        first += count


def sums_of(chains, half):
    if half < 64:
        return [rows_sum(terms, half) for terms in chains]
    blocks = 4 if half >= 256 else 1
    width = chains[0][0][0].shape[1]
    shape = (half // blocks, width)
    flat = [term for terms in chains for term in terms]

    def spec(index):
        return pl.BlockSpec(shape, lambda i, at: (at[index] * blocks + i, 0))

    starts = jnp.stack([jnp.asarray(at // half, jnp.int32) for _, at in flat])
    return pl.pallas_call(
        functools.partial(sum_kernel, counts=[len(terms) for terms in chains]),
        grid_spec=pltpu.PrefetchScalarGridSpec(
            num_scalar_prefetch=1,
            grid=(blocks,),
            in_specs=[spec(index) for index in range(len(flat))],
            out_specs=[pl.BlockSpec(shape, lambda i, at: (i, 0))] * len(chains),
        ),
        out_shape=[jax.ShapeDtypeStruct((half, width), BF)] * len(chains),
        cost_estimate=small_cost(),
    )(starts, *[array for array, _ in flat])


def spread(values, *axes):
    steps = steps_of(axes)
    if len(steps) != 2:
        for step in steps[:-1]:
            values = values + trade(values, step)
        return [values, trade(values, steps[-1])]
    if len(axes) == 1:
        both = swap(values, axes[0], 3)
    else:
        n = lax.axis_size(axes[1])
        pairs = [(i, (i // n ^ 1) * n + (i % n ^ 1)) for i in range(2 * n)]
        both = lax.ppermute(values, axes, pairs)
    return [values, trade(values, steps[0]), trade(values, steps[1]), both]


def total(parts):
    if len(parts) == 2:
        return parts[0] + parts[1]
    return (parts[0] + parts[1]) + (parts[2] + parts[3])


def reduce_both(chains, steps):
    half = chains[0][-1][0].shape[0] // 2
    owns = [bit_of(step) for step in steps]
    sent = sums_of(
        [[(array, at + (1 - own) * half) for array, at in terms] for terms, own in zip(chains, owns)],
        half,
    )
    kept = [
        [(array, at + own * half) for array, at in terms] + [(trade(went, step), 0)]
        for terms, own, went, step in zip(chains, owns, sent, steps)
    ]
    return kept, sent


def rows_sum(terms, rows):
    parts = [lax.dynamic_slice_in_dim(array, at, rows, 0) for array, at in terms]
    return sum(part.astype(F32) for part in parts).astype(BF)


def summed(chains):
    return sums_of(chains, chains[0][-1][0].shape[0])


def join(share, got, step):
    return ordered(bit_of(step) == 0, share, got, 0)


def gather_step(share, step):
    return join(share, trade(share, step), step)


def body(
    inputs,
    cotangent,
    offsets,
    end_flags,
    ln_gain,
    ln_bias,
    w_query,
    w_key,
    w_value,
    w_proj,
    w_in,
    b_in,
    w_out,
    b_out,
):
    count, rows, width = inputs.shape
    hidden = w_in.shape[1]
    tokens = count * rows
    assert count == lax.axis_size("z")
    z, x, c = (lax.axis_index(axis) for axis in ("z", "x", "core"))
    first_a, first_b = steps_of("x"), steps_of("y")[:1]
    near_a, near_b = steps_of("y"), steps_of("y")[1:] + steps_of("x")
    rest_a, rest_b = near_a + steps_of("z"), near_b + steps_of("Z")
    own_a, own_b = bit_of(first_a[0]), bit_of(first_b[0])
    core = c * 4
    sent = jnp.stack([core + 1 - own_a, core + 3 - own_b]).astype(jnp.int32)
    kept = jnp.stack([core + own_a, core + 2 + own_b]).astype(jnp.int32)

    bounds = jnp.where(end_flags == 1, offsets, 0).astype(F32)
    bounds = jnp.where(x == c, bounds, swap(bounds, "core", 1)).astype(jnp.int32)
    bound = lax.dynamic_index_in_dim(bounds, z, 0, keepdims=False)
    turns = tables(2 * count * rows)

    pair = norm_pair(inputs, cotangent, ln_gain, ln_bias)
    pair_other = swap(pair, "core", 1)
    pair_cross = cross(pair)

    ff_args = (pair, pair_other, w_in, b_in.reshape(1, -1), w_out)
    a_sent, b_sent, act, inner, bias = feed_forward(sent, *ff_args)
    a_got, b_got = trade(a_sent, first_a[0]), trade(b_sent, first_b[0])
    entries = trade_parts(after(pair_cross, bias), z)
    a_kept, b_kept, act_late, inner_late, bias_late = feed_forward(
        after(kept, bias, entries[0], bound), *ff_args
    )
    ff_kept, ff_sent = ff_ends(
        after(jnp.concatenate([sent, kept]), bias_late), act, act_late, inner, inner_late, w_in, w_out
    )

    steps = list(zip(rest_a, rest_b))
    a_got, b_got = after((a_got, b_got), ff_kept)
    ff_terms, went = reduce_both([[(a_kept, 0), (a_got, 0)], [(b_kept, 0), (b_got, 0)]], steps[0])
    held = landed(after(entries, went), z)
    there = swap(held, "core", 1)
    attn_args = ((held, there), w_query, w_key, w_value, w_proj, turns)

    def scalars(*values):
        return jnp.stack([jnp.asarray(value, jnp.int32) for value in values])

    *parts_1, ha_sent = attention(scalars(bound, c, sent[0]), 1, *attn_args)
    ff_terms, ha_sent, ff_sent = after((ff_terms, ha_sent, ff_sent), parts_1)
    ff_terms, went = reduce_both(ff_terms, steps[1])
    ff_other = swap(ff_sent, "core", 1)
    ha_got = trade(ha_sent, first_a[0])
    *parts_2, hb_sent, ha_kept = attention(
        after(scalars(bound, c, sent[1], kept[0]), went), 2, *attn_args
    )
    ff_terms, hb_sent, ff_other = after((ff_terms, hb_sent, ff_other), parts_2)
    ff_terms, went = reduce_both(ff_terms, steps[2])
    hb_got = trade(hb_sent, first_b[0])
    *parts_3, hb_kept = attention(after(scalars(bound, c, kept[1]), went, ff_other), 1, *attn_args)
    ff_terms = after(ff_terms, hb_kept)
    for step in steps[3:]:
        ff_terms, _ = reduce_both(ff_terms, step)
    far, near = steps[len(near_a) :], steps[: len(near_a)]
    ff_sums = summed(ff_terms)

    def grown(sums, step):
        return [gather_step(share, one) for share, one in zip(sums, step)]

    got = [trade(sums, step) for sums, step in zip(ff_sums, far[-1])]
    terms = after([[(ha_kept, 0), (ha_got, 0)], [(hb_kept, 0), (hb_got, 0)]], ff_sums)
    terms, went = reduce_both(terms, steps[0])
    heads_kept, heads_sent = heads_ends(
        after(scalars(c, sent[0], sent[1], kept[0], kept[1]), went),
        (parts_1, parts_2, parts_3), held.shape, w_query, w_key, w_value, w_proj,
    )
    got, terms, heads_sent = after((got, terms, heads_sent), heads_kept)
    for after_step, step in zip(far[:0:-1], far[-2::-1]):
        ff_sums = [join(*one) for one in zip(ff_sums, got, after_step)]
        got = [trade(sums, one) for sums, one in zip(ff_sums, step)]
    heads_other = swap(after(heads_sent, ff_sums), "core", 1)
    out_cross, back_cross = (
        cross((heads_kept[:, i] + heads_other[:, i].astype(F32)).astype(BF)) for i in range(2)
    )
    got = after(got, out_cross, back_cross)
    ff_sums = [join(*one) for one in zip(ff_sums, got, far[0])]
    share = jnp.concatenate(ff_sums, axis=0)
    ff_parts = lax.all_gather(share, ("x", "y", "core"), axis=0, tiled=False)
    terms, back_cross = after((terms, back_cross), share)
    terms, went = reduce_both(terms, steps[1])
    heads_back = trade_z(after(back_cross, went))
    for step in steps[2:]:
        terms, _ = reduce_both(terms, step)
    sums = summed(after(terms))
    got = [trade(share, one) for share, one in zip(sums, far[-1])]
    heads_back = after(heads_back, sums)

    ff = (ff_kept + ff_other.astype(F32)).reshape(2, count, rows, width)
    full_in, grad_full = inputs.astype(F32), cotangent.astype(F32)
    _, norm_back = jax.vjp(layernorm, full_in, ln_gain, ln_bias)
    grad_flat, grad_ln_gain, grad_ln_bias = norm_back(ff[1] + heads_back.astype(F32))
    grad_inputs = grad_full + grad_flat

    grad_b_in = jnp.zeros((8, hidden // 8), F32)
    for units, rows_of in ((sent, bias), (kept, bias_late)):
        for i in range(2):
            part = rows_of[:, i * hidden // 8 : (i + 1) * hidden // 8]
            grad_b_in = lax.dynamic_update_slice_in_dim(grad_b_in, part, units[i], 0)
    small = jnp.concatenate(
        [grad_ln_gain, grad_ln_bias, grad_b_in.reshape(-1), jnp.sum(grad_full, axis=(0, 1))]
    ).reshape(-1, LANES)
    sums = [join(*one) for one in zip(sums, after(got, small), far[-1])]
    for step in far[-2::-1]:
        small = after(small, sums)
        sums = grown(sums, step)
    small = total(spread(small, "z"))
    small = total(spread(small, "core"))
    heads_out = trade_z(after(out_cross, sums, small))

    sums, ff_parts, small = after((sums, ff_parts, small))
    small = spread(small, "x", "y")
    for step in near[:0:-1]:
        sums = grown(sums, step)
    got = [trade(share, step) for share, step in zip(sums, near[0])]
    got, small = after((got, small))
    sums = [join(*one) for one in zip(sums, got, near[0])]
    distant = [trade(share, step[0]) for share, step in zip(sums, (first_a, first_b))]
    other = [swap(share, "core", 1) for share in sums]
    orders = (first_a + near_a, first_b + near_b)
    sum_w_out, sum_w_in = place_ff(after(ff_parts, sums), orders)
    heads_out = after(heads_out, sum_w_out).astype(F32)
    outputs = (full_in + heads_out + ff[0] + b_out).astype(BF)
    across = jnp.stack([4 - 2 * core] * 2)
    filled = place_heads(
        jnp.concatenate([kept, kept + across]), sums + after(other, sum_w_out)
    )
    distant = after(distant, filled)
    sum_query, sum_key, sum_value, sum_proj = place_heads(
        jnp.concatenate([sent, sent + across]),
        distant + [swap(share, "core", 1) for share in distant],
        filled,
    )
    small = total(small)
    sum_ln_gain, sum_ln_bias, sum_b_in, sum_b_out = jnp.split(
        small.reshape(-1), [width, 2 * width, 2 * width + hidden]
    )
    return (
        outputs,
        grad_inputs,
        sum_ln_gain,
        sum_ln_bias,
        sum_query,
        sum_key,
        sum_value,
        sum_proj,
        sum_w_in.reshape(width, hidden),
        sum_b_in,
        sum_w_out,
        sum_b_out,
    )


def solution(mesh):
    n_seq, n_win = mesh.devices.shape
    fine = jax.sharding.Mesh(
        mesh.devices.reshape(n_seq // 2, 2, n_win // 2, 2), ("z", "x", "y", "core")
    )
    win, seq = ("y", "core"), ("z", "x")
    cube = P(win, seq, None)
    return jax.shard_map(
        body,
        mesh=fine,
        in_specs=(cube, cube, P(win), P(win)) + (P(),) * 10,
        out_specs=(cube, cube) + (P(),) * 10,
        check_vma=False,
    )
```

```python
import functools
import math

import jax
import jax.numpy as jnp
import numpy as np
from jax import lax
from jax.experimental import pallas as pl
from jax.experimental.pallas import tpu as pltpu
from jax.sharding import PartitionSpec as P

HEAD_DIM = 64
ROT = 32
LANES = 128
BF = jnp.bfloat16
F32 = jnp.float32


def tables(count):
    column = np.arange(LANES) % HEAD_DIM
    frequency = np.exp((column // 2) * (-2.0 * math.log(10000.0) / ROT)).astype(np.float32)
    angles = (np.arange(count, dtype=np.float32)[:, None] * frequency).astype(np.float64)
    rotated = column < ROT
    even = column % 2 == 0
    cosine = np.where(rotated, np.cos(angles), 1.0)
    sine = np.where(rotated, np.sin(angles), 0.0)
    ahead = np.where(even, -sine, 0.0)
    behind = np.where(even, 0.0, sine)
    return [jnp.asarray(table, F32) for table in (cosine, ahead, behind)]


def layernorm(values, gain, shift):
    center = values - jnp.mean(values, axis=-1, keepdims=True)
    spread = jnp.mean(center * center, axis=-1, keepdims=True)
    return center * lax.rsqrt(spread + 1e-05) * gain + shift


def norm_kernel(inputs_ref, grad_ref, gain_ref, bias_ref, pair_ref):
    values = inputs_ref[0].astype(F32)
    pair_ref[0, 0] = layernorm(values, gain_ref[...], bias_ref[...]).astype(BF)
    pair_ref[0, 1] = grad_ref[0]


def norm_pair(inputs, cotangent, gain, bias):
    count, rows, width = inputs.shape
    cube = pl.BlockSpec((1, rows, width), lambda i: (i, 0, 0))
    return pl.pallas_call(
        norm_kernel,
        grid=(count,),
        in_specs=[cube, cube, whole((1, width)), whole((1, width))],
        out_specs=pl.BlockSpec((1, 2, rows, width), lambda i: (i, 0, 0, 0)),
        out_shape=jax.ShapeDtypeStruct((count, 2, rows, width), BF),
        cost_estimate=small_cost(),
    )(inputs, cotangent, gain.reshape(1, -1), bias.reshape(1, -1))


def dot(left, right, left_dim=1, right_dim=0):
    return lax.dot_general(
        left, right, (((left_dim,), (right_dim,)), ((), ())), preferred_element_type=F32
    )


def after(values, *gates):
    return lax.optimization_barrier((values, gates))[0]


def small_cost():
    return pl.CostEstimate(flops=1 << 20, bytes_accessed=1 << 16, transcendentals=0)


def whole(shape):
    return pl.BlockSpec(shape, lambda *at: (0,) * len(shape))


def gelu_both(values):
    scale, cubic = math.sqrt(2.0 / math.pi), 0.044715
    square = values * values
    tanh = jnp.tanh(scale * values * (1.0 + cubic * square))
    half = 0.5 * (1.0 + tanh)
    slope = half + 0.5 * scale * values * (1.0 - tanh * tanh) * (1.0 + 3.0 * cubic * square)
    return values * half, slope


def ff_kernel(
    units_ref, own_ref, other_ref, w_in_ref, b_in_ref, w_out_ref,
    first_ref, second_ref, act_ref, inner_ref, bias_ref,
    normed, grad, normed_turned,
):
    step = pl.program_id(0)
    count, _, rows, _ = own_ref.shape

    @pl.when(step == 0)
    def _():
        for place, ref in enumerate((own_ref, other_ref)):
            for i in range(count):
                at = slice((place * count + i) * rows, (place * count + i + 1) * rows)
                normed[at] = ref[i, 0]
                grad[at] = ref[i, 1]
        normed_turned[...] = normed[...].T

    act, slope = gelu_both(dot(normed[...], w_in_ref[...]) + b_in_ref[...])
    act = act.astype(BF)
    act_ref[...] = act
    grad_inner = (dot(grad[...], w_out_ref[...], 1, 1) * slope).astype(BF)
    inner_ref[...] = grad_inner
    bias_ref[...] = jnp.sum(grad_inner.astype(F32), axis=0, keepdims=True)
    units = act.shape[1]
    grad_w_out = dot(act, grad[...], 0, 0).astype(BF)
    grad_w_in = dot(normed_turned[...], grad_inner).astype(BF)

    def store(ref):
        ref[:units] = grad_w_out
        ref[units:, :units] = grad_w_in[:units]
        ref[units:, units:] = grad_w_in[units:]

    pl.when(step == 0)(lambda: store(first_ref))
    pl.when(step == 1)(lambda: store(second_ref))


def feed_forward(units, own, other, w_in, b_in, w_out):
    tokens, width = own.shape[0] * own.shape[2], own.shape[3]
    size = w_in.shape[1] // 8
    block = pl.BlockSpec((2 * tokens, size), lambda step, units: (0, step))
    return pl.pallas_call(
        ff_kernel,
        grid_spec=pltpu.PrefetchScalarGridSpec(
            num_scalar_prefetch=1,
            grid=(2,),
            in_specs=[whole(own.shape)] * 2
            + [
                pl.BlockSpec((width, size), lambda step, units: (0, units[step])),
                pl.BlockSpec((1, size), lambda step, units: (0, units[step])),
                pl.BlockSpec((size, width), lambda step, units: (units[step], 0)),
            ],
            out_specs=[whole((2 * size, width))] * 2
            + [block, block, pl.BlockSpec((1, size), lambda step, units: (0, step))],
            scratch_shapes=[
                pltpu.VMEM((2 * tokens, width), BF),
                pltpu.VMEM((2 * tokens, width), BF),
                pltpu.VMEM((width, 2 * tokens), BF),
            ],
        ),
        out_shape=[jax.ShapeDtypeStruct((2 * size, width), BF)] * 2
        + [jax.ShapeDtypeStruct((2 * tokens, 2 * size), BF)] * 2
        + [jax.ShapeDtypeStruct((1, 2 * size), F32)],
        compiler_params=pltpu.CompilerParams(vmem_limit_bytes=56 << 20),
        cost_estimate=small_cost(),
    )(units, own, other, w_in, b_in, w_out)


def ff_late_kernel(
    units_ref, own_ref, other_ref, act_ref, inner_ref, w_in_ref, b_in_ref, w_out_ref,
    first_ref, second_ref, bias_ref, kept, sent,
    normed, grad, normed_turned, out_sum, back_sum,
):
    step = pl.program_id(0)
    count, _, rows, _ = own_ref.shape
    tokens = count * rows
    size = w_in_ref.shape[1]

    @pl.when(step == 0)
    def _():
        for place, ref in enumerate((own_ref, other_ref)):
            for i in range(count):
                at = slice((place * count + i) * rows, (place * count + i + 1) * rows)
                normed[at] = ref[i, 0]
                grad[at] = ref[i, 1]
        normed_turned[...] = normed[...].T

    def add(act, grad_inner):
        out = dot(act, w_out_ref[...])
        back = dot(grad_inner, w_in_ref[...], 1, 1)

        @pl.when(step == 0)
        def _():
            out_sum[...] = out
            back_sum[...] = back

        @pl.when(step > 0)
        def _():
            out_sum[...] += out
            back_sum[...] += back

    @pl.when(step < 2)
    def _():
        act, slope = gelu_both(dot(normed[...], w_in_ref[...]) + b_in_ref[...])
        act = act.astype(BF)
        grad_inner = (dot(grad[...], w_out_ref[...], 1, 1) * slope).astype(BF)
        bias_ref[...] = jnp.sum(grad_inner.astype(F32), axis=0, keepdims=True)
        grad_w_out = dot(act, grad[...], 0, 0).astype(BF)
        grad_w_in = dot(normed_turned[...], grad_inner).astype(BF)

        def store(ref):
            ref[:size] = grad_w_out
            ref[size:, :size] = grad_w_in[:size]
            ref[size:, size:] = grad_w_in[size:]

        pl.when(step == 0)(lambda: store(first_ref))
        pl.when(step == 1)(lambda: store(second_ref))
        add(act, grad_inner)

    for i in range(2):

        @pl.when(step == 2 + i)
        def _():
            cols = slice(i * size, (i + 1) * size)
            add(act_ref[:, cols], inner_ref[:, cols])

    @pl.when(step == 3)
    def _():
        for i, sums in enumerate((out_sum, back_sum)):
            kept[i] = sums[:tokens]
            sent[i] = sums[tokens:].astype(BF)


def feed_forward_late(units, own, other, w_in, b_in, w_out, act, inner):
    tokens, width = own.shape[0] * own.shape[2], own.shape[3]
    size = w_in.shape[1] // 8

    def once(shape):
        return pl.BlockSpec(
            shape, lambda *at: (0,) * len(shape), pipeline_mode=pl.Buffered(1)
        )

    return pl.pallas_call(
        ff_late_kernel,
        grid_spec=pltpu.PrefetchScalarGridSpec(
            num_scalar_prefetch=1,
            grid=(4,),
            in_specs=[once(own.shape)] * 2
            + [once(act.shape)] * 2
            + [
                pl.BlockSpec((width, size), lambda step, units: (0, units[step])),
                pl.BlockSpec((1, size), lambda step, units: (0, units[step])),
                pl.BlockSpec((size, width), lambda step, units: (units[step], 0)),
            ],
            out_specs=[whole((2 * size, width))] * 2
            + [pl.BlockSpec((1, size), lambda step, units: (0, jnp.minimum(step, 1)))]
            + [whole((2, tokens, width))] * 2,
            scratch_shapes=[
                pltpu.VMEM((2 * tokens, width), BF),
                pltpu.VMEM((2 * tokens, width), BF),
                pltpu.VMEM((width, 2 * tokens), BF),
            ]
            + [pltpu.VMEM((2 * tokens, width), F32)] * 2,
        ),
        out_shape=[jax.ShapeDtypeStruct((2 * size, width), BF)] * 2
        + [
            jax.ShapeDtypeStruct((1, 2 * size), F32),
            jax.ShapeDtypeStruct((2, tokens, width), F32),
            jax.ShapeDtypeStruct((2, tokens, width), BF),
        ],
        compiler_params=pltpu.CompilerParams(vmem_limit_bytes=62 << 20),
        cost_estimate=small_cost(),
    )(units, own, other, act, inner, w_in, b_in, w_out)


def attend(bound, query, key, value, grad, rotate_back, scratch, block):
    k_turned, v_turned, mixed_turned, gq_turned, gk_sum, gv_sum = scratch
    count, lanes = query.shape
    k_turned[...] = key.T
    v_turned[...] = value.T
    gk_sum[...] = jnp.zeros_like(gk_sum)
    gv_sum[...] = jnp.zeros_like(gv_sum)
    lane = lax.broadcasted_iota(jnp.int32, (count, lanes), 1)
    for head in range(lanes // HEAD_DIM):
        cols = slice(head * HEAD_DIM, (head + 1) * HEAD_DIM)
        mine = (lane >= head * HEAD_DIM) & (lane < (head + 1) * HEAD_DIM)
        q_head = jnp.where(mine, query, jnp.zeros_like(query))
        g_head = jnp.where(mine, grad, jnp.zeros_like(grad))
        for start in range(0, count, block):
            seen = start + block
            rows = slice(start, seen)
            scores = dot(key[:seen], q_head[rows], 1, 1)
            at_key = lax.broadcasted_iota(jnp.int32, (seen, block), 0)
            at_query = lax.broadcasted_iota(jnp.int32, (1, block), 1) + start
            lowest = jnp.where(at_query >= bound, bound, 0)
            scores = jnp.where((at_key <= at_query) & (at_key >= lowest), scores, -1e30)
            probs = jnp.exp(scores - jnp.max(scores, axis=0, keepdims=True))
            probs = probs * (1.0 / jnp.sum(probs, axis=0, keepdims=True))
            probs_low = probs.astype(BF)
            grad_probs = dot(value[:seen], g_head[rows], 1, 1)
            row_dot = jnp.sum(probs * grad_probs, axis=0, keepdims=True)
            grad_scores = (probs * (grad_probs - row_dot)).astype(BF)
            mixed_turned[cols, rows] = dot(v_turned[cols, :seen], probs_low)
            gq_turned[cols, rows] = dot(k_turned[cols, :seen], grad_scores)
            gv_sum[:seen, :] += dot(probs_low, g_head[rows])
            gk_sum[:seen, :] += dot(grad_scores, q_head[rows])
    grad_query = (gq_turned[...].T * HEAD_DIM ** -0.5).astype(BF).astype(F32)
    return (
        rotate_back(grad_query).astype(BF),
        rotate_back(gk_sum[...].astype(BF).astype(F32)).astype(BF),
        gv_sum[...].astype(BF),
    )


def heads_kernel(
    scalars_ref, held, there, w_q_ref, w_k_ref, w_v_ref, w_p_ref, cos_ref, ahead_ref, behind_ref,
    mixed_ref, grads_ref, *rest, pairs, block,
):
    sums, (normed_ref, grad_ref, normed_turned), scratch = (
        rest[:pairs], rest[pairs : pairs + 3], rest[pairs + 3 :]
    )
    step = pl.program_id(0)
    bound, core = scalars_ref[0], scalars_ref[1]
    count, width = normed_ref.shape
    chunks, _, rows, _ = held.shape
    lanes = w_q_ref.shape[1]
    cosine, ahead, behind = cos_ref[...], ahead_ref[...], behind_ref[...]

    def at(index):
        return pl.ds(pl.multiple_of(index * rows, rows), rows)

    def rotate(values):
        return (
            values * cosine
            + pltpu.roll(values, lanes - 1, 1) * ahead
            + pltpu.roll(values, 1, 1) * behind
        )

    def rotate_back(grads):
        return (
            grads * cosine
            + pltpu.roll(grads * ahead, 1, 1)
            + pltpu.roll(grads * behind, lanes - 1, 1)
        )

    @pl.when(step == 0)
    def _():
        for i in range(chunks):
            mine, other = at(2 * i + core), at(2 * i + 1 - core)
            normed_ref[mine, :] = held[i, 0]
            normed_ref[other, :] = there[i, 0]
            grad_ref[mine, :] = held[i, 1]
            grad_ref[other, :] = there[i, 1]
        normed_turned[...] = normed_ref[...].T

    weights = jnp.concatenate([w_q_ref[...], w_k_ref[...], w_v_ref[...]], axis=1)
    raw = dot(normed_ref[...], weights)
    query = (rotate(raw[:, :lanes]).astype(BF).astype(F32) * HEAD_DIM ** -0.5).astype(BF)
    key = rotate(raw[:, lanes : 2 * lanes]).astype(BF)
    value = raw[:, 2 * lanes :].astype(BF)
    grad_mixed = dot(grad_ref[...], w_p_ref[...], 1, 1).astype(BF)
    parts = attend(bound, query, key, value, grad_mixed, rotate_back, scratch, block)
    mixed_turned = scratch[2][...].astype(BF)
    mixed_ref[...] = mixed_turned.T
    grads = jnp.concatenate(parts, axis=1)
    grads_ref[...] = grads
    grad_weights = dot(normed_turned[...], grads).astype(BF)
    grad_proj = dot(mixed_turned, grad_ref[...]).astype(BF)

    def store(ref):
        ref[:lanes] = grad_proj
        for i in range(3):
            for j in range(width // lanes):
                ref[(i + 1) * lanes : (i + 2) * lanes, j * lanes : (j + 1) * lanes] = grad_weights[
                    j * lanes : (j + 1) * lanes, i * lanes : (i + 1) * lanes
                ]

    for i in range(pairs):
        pl.when(step == i)(functools.partial(store, sums[i]))


def attention(scalars, pairs, window, w_query, w_key, w_value, w_proj, turns):
    chunks, _, rows, width = window[0].shape
    count = 2 * chunks * rows
    cols = pl.BlockSpec((width, LANES), lambda step, s: (0, s[2 + step]))
    sums = jax.ShapeDtypeStruct((4 * LANES, width), BF)
    return pl.pallas_call(
        functools.partial(heads_kernel, pairs=pairs, block=512),
        grid_spec=pltpu.PrefetchScalarGridSpec(
            num_scalar_prefetch=1,
            grid=(pairs,),
            in_specs=[whole(window[0].shape)] * 2
            + [cols] * 3
            + [pl.BlockSpec((LANES, width), lambda step, s: (s[2 + step], 0))]
            + [whole((count, LANES))] * 3,
            out_specs=[
                pl.BlockSpec((count, LANES), lambda step, s: (0, step)),
                pl.BlockSpec((count, 3 * LANES), lambda step, s: (0, step)),
            ]
            + [whole(sums.shape)] * pairs,
            scratch_shapes=[
                pltpu.VMEM((count, width), BF),
                pltpu.VMEM((count, width), BF),
                pltpu.VMEM((width, count), BF),
            ]
            + [pltpu.VMEM((LANES, count), BF)] * 2
            + [pltpu.VMEM((LANES, count), F32)] * 2
            + [pltpu.VMEM((count, LANES), F32)] * 2,
        ),
        out_shape=[
            jax.ShapeDtypeStruct((count, pairs * LANES), BF),
            jax.ShapeDtypeStruct((count, 3 * pairs * LANES), BF),
        ]
        + [sums] * pairs,
        compiler_params=pltpu.CompilerParams(vmem_limit_bytes=60 << 20),
        cost_estimate=small_cost(),
    )(scalars, *window, w_query, w_key, w_value, w_proj, *turns)


def heads_ends_kernel(
    scalars_ref, *refs, calls,
):
    tensors, (w_q, w_k, w_v, w_p, kept, sent, out_sum, back_sum) = refs[: 2 * calls], refs[2 * calls :]
    step = pl.program_id(0)
    core = scalars_ref[0]
    chunks, _, rows, _ = kept.shape
    first = 0
    for call in range(calls):
        mixed, grads = tensors[2 * call : 2 * call + 2]
        for i in range(mixed.shape[1] // LANES):

            @pl.when(step == first + i)
            def _():
                weights = jnp.concatenate([w_q[...], w_k[...], w_v[...]], axis=1)
                out = dot(mixed[:, i * LANES : (i + 1) * LANES], w_p[...])
                back = dot(grads[:, 3 * i * LANES : 3 * (i + 1) * LANES], weights, 1, 1)
                if first + i == 0:
                    out_sum[...] = out
                    back_sum[...] = back
                else:
                    out_sum[...] += out
                    back_sum[...] += back

        first += mixed.shape[1] // LANES

    @pl.when(step == first - 1)
    def _():
        for i in range(chunks):
            for j, sums in enumerate((out_sum, back_sum)):
                mine = pl.ds(pl.multiple_of((2 * i + core) * rows, rows), rows)
                other = pl.ds(pl.multiple_of((2 * i + 1 - core) * rows, rows), rows)
                kept[i, j] = sums[mine, :]
                sent[i, j] = sums[other, :].astype(BF)


def heads_ends(scalars, parts, shape, w_query, w_key, w_value, w_proj):
    count, width = parts[0][0].shape[0], w_query.shape[0]
    pairs = sum(mixed.shape[1] for mixed, _ in parts) // LANES
    tensors = [tensor for part in parts for tensor in part]
    cols = pl.BlockSpec((width, LANES), lambda step, s: (0, s[1 + step]))
    return pl.pallas_call(
        functools.partial(heads_ends_kernel, calls=len(parts)),
        grid_spec=pltpu.PrefetchScalarGridSpec(
            num_scalar_prefetch=1,
            grid=(pairs,),
            in_specs=[whole(tensor.shape) for tensor in tensors]
            + [cols] * 3
            + [pl.BlockSpec((LANES, width), lambda step, s: (s[1 + step], 0))],
            out_specs=[whole(shape)] * 2,
            scratch_shapes=[pltpu.VMEM((count, width), F32)] * 2,
        ),
        out_shape=[jax.ShapeDtypeStruct(shape, F32), jax.ShapeDtypeStruct(shape, BF)],
        compiler_params=pltpu.CompilerParams(vmem_limit_bytes=60 << 20),
        cost_estimate=small_cost(),
    )(scalars, *tensors, w_query, w_key, w_value, w_proj)


def place_ff_kernel(out_ref, in_ref, w_out_ref, w_in_ref):
    size = w_in_ref.shape[2]
    w_out_ref[...] = out_ref[0].astype(F32)
    both = in_ref[0].astype(F32)
    w_in_ref[0] = both[:, :size]
    w_in_ref[1] = both[:, size:]


def device_of(core, index, steps):
    at = {"x": 0, "y": 0}
    for place, (axis, bit) in enumerate(steps):
        at[axis] = at[axis] + (index // 2 ** (len(steps) - 1 - place)) % 2 * 2**bit
    return (at["x"] * lax.axis_size("y") + at["y"]) * 2 + core


def place_ff(parts, orders):
    devices, held, width = parts.shape
    held, size = held // 2, width // 2
    rows = min(size, held)
    chunks = size // rows

    def split(step):
        return step // (4 * chunks), step // (2 * chunks) % 2, step // chunks % 2, step % chunks

    def source(step, of_in):
        core, chain, first, chunk = split(step)
        row = of_in * size + chunk * rows
        index = first * (width // held) + row // held
        a_side, b_side = (device_of(core, index, steps) for steps in orders)
        return (jnp.where(chain == 0, a_side, b_side), (chain * held + row % held) // rows, 0)

    def block_of(step):
        core, chain, first, chunk = split(step)
        return core * 4 + chain * 2 + first, chunk

    return pl.pallas_call(
        place_ff_kernel,
        grid=(8 * chunks,),
        in_specs=[
            pl.BlockSpec((1, rows, width), lambda step: source(step, 0)),
            pl.BlockSpec((1, rows, width), lambda step: source(step, 1)),
        ],
        out_specs=[
            pl.BlockSpec(
                (rows, width), lambda step: (block_of(step)[0] * chunks + block_of(step)[1], 0)
            ),
            pl.BlockSpec((2, rows, size), lambda step: (0, block_of(step)[1], block_of(step)[0])),
        ],
        out_shape=[
            jax.ShapeDtypeStruct((8 * size, width), F32),
            jax.ShapeDtypeStruct((2, size, 8 * size), F32),
        ],
        compiler_params=pltpu.CompilerParams(vmem_limit_bytes=60 << 20),
        cost_estimate=small_cost(),
    )(parts, parts)


def place_heads_kernel(pairs_ref, a_ref, b_ref, c_ref, d_ref, *rest):
    q_out, k_out, v_out, p_out = rest[-4:]
    lanes, width = p_out.shape
    for index, ref in enumerate((a_ref, b_ref, c_ref, d_ref)):

        @pl.when(pl.program_id(0) == index)
        def _():
            p_out[...] = ref[:lanes].astype(F32)
            for i, out in enumerate((q_out, k_out, v_out)):
                for j in range(width // lanes):
                    out[j * lanes : (j + 1) * lanes, :] = ref[
                        (i + 1) * lanes : (i + 2) * lanes, j * lanes : (j + 1) * lanes
                    ].astype(F32)


def place_heads(pairs, sums, filled=()):
    width = sums[0].shape[1]
    cols = pl.BlockSpec((width, LANES), lambda step, pairs: (0, pairs[step]))
    return pl.pallas_call(
        place_heads_kernel,
        grid_spec=pltpu.PrefetchScalarGridSpec(
            num_scalar_prefetch=1,
            grid=(4,),
            in_specs=[whole(sums[0].shape)] * 4
            + [pl.BlockSpec(memory_space=pl.ANY)] * len(filled),
            out_specs=[cols] * 3
            + [pl.BlockSpec((LANES, width), lambda step, pairs: (pairs[step], 0))],
        ),
        out_shape=[jax.ShapeDtypeStruct((width, width), F32)] * 4,
        input_output_aliases={5 + i: i for i in range(len(filled))},
        compiler_params=pltpu.CompilerParams(vmem_limit_bytes=60 << 20),
        cost_estimate=small_cost(),
    )(pairs, *sums, *filled)


def swap(values, axis, bits):
    return lax.ppermute(
        values, axis, [(i, i ^ bits) for i in range(lax.axis_size(axis))]
    )


def cross(values):
    return values, lax.ppermute(values, ("x", "core"), [(1, 2), (2, 1)])


def crossed(pair):
    return jnp.where(lax.axis_index("x") == lax.axis_index("core"), *pair)


def trade_z(cubes):
    return lax.all_to_all(crossed(cubes), "z", split_axis=0, concat_axis=0, tiled=True)


def trade_parts(cubes, z):
    def entry(k):
        at = [lax.dynamic_index_in_dim(cube, z ^ k, 0, keepdims=True) for cube in cubes]
        return crossed(at)

    count = cubes[0].shape[0]
    return [entry(0)] + [swap(entry(k), "z", k) for k in range(1, count)]


def land_kernel(z_ref, *refs):
    for k in range(len(refs) - 1):

        @pl.when(pl.program_id(0) == k)
        def _():
            refs[-1][...] = refs[k][...]


def landed(entries, z):
    count = len(entries)
    shape = entries[0].shape
    return pl.pallas_call(
        land_kernel,
        grid_spec=pltpu.PrefetchScalarGridSpec(
            num_scalar_prefetch=1,
            grid=(count,),
            in_specs=[whole(shape)] * count,
            out_specs=pl.BlockSpec(shape, lambda k, z: (z[0] ^ k, 0, 0, 0)),
        ),
        out_shape=jax.ShapeDtypeStruct((count,) + shape[1:], BF),
        cost_estimate=small_cost(),
    )(z.reshape(1), *entries)


def ordered(first_is_own, own, other, axis):
    return jnp.where(
        first_is_own,
        jnp.concatenate([own, other], axis=axis),
        jnp.concatenate([other, own], axis=axis),
    )


def steps_of(order):
    found = []
    for letter in order:
        bits = [(letter.lower(), b) for b in range(lax.axis_size(letter.lower()).bit_length() - 1)]
        found += bits[::-1] if letter == "Z" else bits
    return found


def bit_of(step):
    axis, bit = step
    return (lax.axis_index(axis) >> bit) & 1


def trade(values, step):
    axis, bit = step
    return swap(values, axis, 1 << bit)


def sum_kernel(at_ref, *refs, counts):
    first = 0
    for count, out in zip(counts, refs[sum(counts) :]):
        out[...] = sum(ref[...].astype(F32) for ref in refs[first : first + count]).astype(BF)
        first += count


def sums_of(chains, half):
    if half < 64:
        return [rows_sum(terms, half) for terms in chains]
    blocks = 4 if half >= 256 else 1
    width = chains[0][0][0].shape[1]
    shape = (half // blocks, width)
    flat = [term for terms in chains for term in terms]

    def spec(index):
        return pl.BlockSpec(shape, lambda i, at: (at[index] * blocks + i, 0))

    starts = jnp.stack([jnp.asarray(at // half, jnp.int32) for _, at in flat])
    return pl.pallas_call(
        functools.partial(sum_kernel, counts=[len(terms) for terms in chains]),
        grid_spec=pltpu.PrefetchScalarGridSpec(
            num_scalar_prefetch=1,
            grid=(blocks,),
            in_specs=[spec(index) for index in range(len(flat))],
            out_specs=[pl.BlockSpec(shape, lambda i, at: (i, 0))] * len(chains),
        ),
        out_shape=[jax.ShapeDtypeStruct((half, width), BF)] * len(chains),
        cost_estimate=small_cost(),
    )(starts, *[array for array, _ in flat])


def spread(values, *axes):
    steps = steps_of(axes)
    if len(steps) != 2:
        for step in steps[:-1]:
            values = values + trade(values, step)
        return [values, trade(values, steps[-1])]
    if len(axes) == 1:
        both = swap(values, axes[0], 3)
    else:
        n = lax.axis_size(axes[1])
        pairs = [(i, (i // n ^ 1) * n + (i % n ^ 1)) for i in range(2 * n)]
        both = lax.ppermute(values, axes, pairs)
    return [values, trade(values, steps[0]), trade(values, steps[1]), both]


def total(parts):
    if len(parts) == 2:
        return parts[0] + parts[1]
    return (parts[0] + parts[1]) + (parts[2] + parts[3])


def reduce_both(chains, steps):
    half = chains[0][-1][0].shape[0] // 2
    owns = [bit_of(step) for step in steps]
    sent = sums_of(
        [[(array, at + (1 - own) * half) for array, at in terms] for terms, own in zip(chains, owns)],
        half,
    )
    kept = [
        [(array, at + own * half) for array, at in terms] + [(trade(went, step), 0)]
        for terms, own, went, step in zip(chains, owns, sent, steps)
    ]
    return kept, sent


def rows_sum(terms, rows):
    parts = [lax.dynamic_slice_in_dim(array, at, rows, 0) for array, at in terms]
    return sum(part.astype(F32) for part in parts).astype(BF)


def summed(chains):
    return sums_of(chains, chains[0][-1][0].shape[0])


def join(share, got, step):
    return ordered(bit_of(step) == 0, share, got, 0)


def gather_step(share, step):
    return join(share, trade(share, step), step)


def body(
    inputs,
    cotangent,
    offsets,
    end_flags,
    ln_gain,
    ln_bias,
    w_query,
    w_key,
    w_value,
    w_proj,
    w_in,
    b_in,
    w_out,
    b_out,
):
    count, rows, width = inputs.shape
    hidden = w_in.shape[1]
    tokens = count * rows
    assert count == lax.axis_size("z")
    z, x, c = (lax.axis_index(axis) for axis in ("z", "x", "core"))
    first_a, first_b = steps_of("x"), steps_of("y")[:1]
    near_a, near_b = steps_of("y"), steps_of("y")[1:] + steps_of("x")
    rest_a, rest_b = near_a + steps_of("z"), near_b + steps_of("Z")
    own_a, own_b = bit_of(first_a[0]), bit_of(first_b[0])
    core = c * 4
    sent = jnp.stack([core + 1 - own_a, core + 3 - own_b]).astype(jnp.int32)
    kept = jnp.stack([core + own_a, core + 2 + own_b]).astype(jnp.int32)

    bounds = jnp.where(end_flags == 1, offsets, 0).astype(F32)
    bounds = jnp.where(x == c, bounds, swap(bounds, "core", 1)).astype(jnp.int32)
    bound = lax.dynamic_index_in_dim(bounds, z, 0, keepdims=False)
    turns = tables(2 * count * rows)

    pair = norm_pair(inputs, cotangent, ln_gain, ln_bias)
    pair_other = swap(pair, "core", 1)
    pair_cross = cross(pair)

    ff_args = (pair, pair_other, w_in, b_in.reshape(1, -1), w_out)
    a_sent, b_sent, act, inner, bias = feed_forward(sent, *ff_args)
    a_got, b_got = trade(a_sent, first_a[0]), trade(b_sent, first_b[0])
    entries = trade_parts(after(pair_cross, bias), z)
    a_kept, b_kept, bias_late, ff_kept, ff_sent = feed_forward_late(
        after(jnp.concatenate([kept, sent]), bias, entries[0]), *ff_args, act, inner
    )

    steps = list(zip(rest_a, rest_b))
    a_got, b_got = after((a_got, b_got), ff_kept)
    ff_terms, went = reduce_both([[(a_kept, 0), (a_got, 0)], [(b_kept, 0), (b_got, 0)]], steps[0])
    held = landed(after(entries, went), z)
    there = swap(held, "core", 1)
    attn_args = ((held, there), w_query, w_key, w_value, w_proj, turns)

    def scalars(*values):
        return jnp.stack([jnp.asarray(value, jnp.int32) for value in values])

    *parts_1, ha_sent = attention(scalars(bound, c, sent[0]), 1, *attn_args)
    ff_terms, ha_sent, ff_sent = after((ff_terms, ha_sent, ff_sent), parts_1)
    ff_terms, went = reduce_both(ff_terms, steps[1])
    ff_other = swap(ff_sent, "core", 1)
    ha_got = trade(ha_sent, first_a[0])
    *parts_2, hb_sent, ha_kept = attention(
        after(scalars(bound, c, sent[1], kept[0]), went), 2, *attn_args
    )
    ff_terms, hb_sent, ff_other = after((ff_terms, hb_sent, ff_other), parts_2)
    ff_terms, went = reduce_both(ff_terms, steps[2])
    hb_got = trade(hb_sent, first_b[0])
    *parts_3, hb_kept = attention(after(scalars(bound, c, kept[1]), went, ff_other), 1, *attn_args)
    ff_terms = after(ff_terms, hb_kept)
    for step in steps[3:]:
        ff_terms, _ = reduce_both(ff_terms, step)
    far, near = steps[len(near_a) :], steps[: len(near_a)]
    ff_sums = summed(ff_terms)

    def grown(sums, step):
        return [gather_step(share, one) for share, one in zip(sums, step)]

    got = [trade(sums, step) for sums, step in zip(ff_sums, far[-1])]
    terms = after([[(ha_kept, 0), (ha_got, 0)], [(hb_kept, 0), (hb_got, 0)]], ff_sums)
    terms, went = reduce_both(terms, steps[0])
    heads_kept, heads_sent = heads_ends(
        after(scalars(c, sent[0], sent[1], kept[0], kept[1]), went),
        (parts_1, parts_2, parts_3), held.shape, w_query, w_key, w_value, w_proj,
    )
    got, terms, heads_sent = after((got, terms, heads_sent), heads_kept)
    for after_step, step in zip(far[:0:-1], far[-2::-1]):
        ff_sums = [join(*one) for one in zip(ff_sums, got, after_step)]
        got = [trade(sums, one) for sums, one in zip(ff_sums, step)]
    heads_other = swap(after(heads_sent, ff_sums), "core", 1)
    out_cross, back_cross = (
        cross((heads_kept[:, i] + heads_other[:, i].astype(F32)).astype(BF)) for i in range(2)
    )
    got = after(got, out_cross, back_cross)
    ff_sums = [join(*one) for one in zip(ff_sums, got, far[0])]
    share = jnp.concatenate(ff_sums, axis=0)
    ff_parts = lax.all_gather(share, ("x", "y", "core"), axis=0, tiled=False)
    terms, back_cross = after((terms, back_cross), share)
    terms, _ = reduce_both(terms, steps[1])
    terms, back_cross = after((terms, back_cross))
    heads_back = trade_z(back_cross)
    for step in steps[2:]:
        terms, _ = reduce_both(terms, step)
    sums = summed(after(terms))
    got = [trade(share, one) for share, one in zip(sums, far[-1])]
    heads_back = after(heads_back, sums)

    ff = (ff_kept + ff_other.astype(F32)).reshape(2, count, rows, width)
    full_in, grad_full = inputs.astype(F32), cotangent.astype(F32)
    _, norm_back = jax.vjp(layernorm, full_in, ln_gain, ln_bias)
    grad_flat, grad_ln_gain, grad_ln_bias = norm_back(ff[1] + heads_back.astype(F32))
    grad_inputs = grad_full + grad_flat

    grad_b_in = jnp.zeros((8, hidden // 8), F32)
    for units, rows_of in ((sent, bias), (kept, bias_late)):
        for i in range(2):
            part = rows_of[:, i * hidden // 8 : (i + 1) * hidden // 8]
            grad_b_in = lax.dynamic_update_slice_in_dim(grad_b_in, part, units[i], 0)
    small = jnp.concatenate(
        [grad_ln_gain, grad_ln_bias, grad_b_in.reshape(-1), jnp.sum(grad_full, axis=(0, 1))]
    ).reshape(-1, LANES)
    sums = [join(*one) for one in zip(sums, after(got, small), far[-1])]
    for step in far[-2::-1]:
        small = after(small, sums)
        sums = grown(sums, step)
    small = total(spread(small, "z"))
    small = total(spread(small, "core"))
    heads_out = trade_z(after(out_cross, sums, small))

    sums, ff_parts, small = after((sums, ff_parts, small))
    small = spread(small, "x", "y")
    for step in near[:0:-1]:
        sums = grown(sums, step)
    got = [trade(share, step) for share, step in zip(sums, near[0])]
    got, small = after((got, small))
    sums = [join(*one) for one in zip(sums, got, near[0])]
    distant = [trade(share, step[0]) for share, step in zip(sums, (first_a, first_b))]
    other = [swap(share, "core", 1) for share in sums]
    orders = (first_a + near_a, first_b + near_b)
    sum_w_out, sum_w_in = place_ff(after(ff_parts, sums), orders)
    heads_out = after(heads_out, sum_w_out).astype(F32)
    outputs = (full_in + heads_out + ff[0] + b_out).astype(BF)
    across = jnp.stack([4 - 2 * core] * 2)
    filled = place_heads(
        jnp.concatenate([kept, kept + across]), sums + after(other, sum_w_out)
    )
    distant = after(distant, filled)
    sum_query, sum_key, sum_value, sum_proj = place_heads(
        jnp.concatenate([sent, sent + across]),
        distant + [swap(share, "core", 1) for share in distant],
        filled,
    )
    small = total(small)
    sum_ln_gain, sum_ln_bias, sum_b_in, sum_b_out = jnp.split(
        small.reshape(-1), [width, 2 * width, 2 * width + hidden]
    )
    return (
        outputs,
        grad_inputs,
        sum_ln_gain,
        sum_ln_bias,
        sum_query,
        sum_key,
        sum_value,
        sum_proj,
        sum_w_in.reshape(width, hidden),
        sum_b_in,
        sum_w_out,
        sum_b_out,
    )


def solution(mesh):
    n_seq, n_win = mesh.devices.shape
    fine = jax.sharding.Mesh(
        mesh.devices.reshape(n_seq // 2, 2, n_win // 2, 2), ("z", "x", "y", "core")
    )
    win, seq = ("y", "core"), ("z", "x")
    cube = P(win, seq, None)
    return jax.shard_map(
        body,
        mesh=fine,
        in_specs=(cube, cube, P(win), P(win)) + (P(),) * 10,
        out_specs=(cube, cube) + (P(),) * 10,
        check_vma=False,
    )
```

```python
import functools
import math

import jax
import jax.numpy as jnp
import numpy as np
from jax import lax
from jax.experimental import pallas as pl
from jax.experimental.pallas import tpu as pltpu
from jax.sharding import PartitionSpec as P

HEAD_DIM = 64
ROT = 32
LANES = 128
BF = jnp.bfloat16
F32 = jnp.float32


def tables(count):
    column = np.arange(LANES) % HEAD_DIM
    frequency = np.exp((column // 2) * (-2.0 * math.log(10000.0) / ROT)).astype(np.float32)
    angles = (np.arange(count, dtype=np.float32)[:, None] * frequency).astype(np.float64)
    rotated = column < ROT
    even = column % 2 == 0
    cosine = np.where(rotated, np.cos(angles), 1.0)
    sine = np.where(rotated, np.sin(angles), 0.0)
    ahead = np.where(even, -sine, 0.0)
    behind = np.where(even, 0.0, sine)
    return [jnp.asarray(table, F32) for table in (cosine, ahead, behind)]


def layernorm(values, gain, shift):
    center = values - jnp.mean(values, axis=-1, keepdims=True)
    spread = jnp.mean(center * center, axis=-1, keepdims=True)
    return center * lax.rsqrt(spread + 1e-05) * gain + shift


def norm_kernel(inputs_ref, grad_ref, gain_ref, bias_ref, pair_ref):
    values = inputs_ref[0].astype(F32)
    pair_ref[0, 0] = layernorm(values, gain_ref[...], bias_ref[...]).astype(BF)
    pair_ref[0, 1] = grad_ref[0]


def norm_pair(inputs, cotangent, gain, bias):
    count, rows, width = inputs.shape
    cube = pl.BlockSpec((1, rows, width), lambda i: (i, 0, 0))
    return pl.pallas_call(
        norm_kernel,
        grid=(count,),
        in_specs=[cube, cube, whole((1, width)), whole((1, width))],
        out_specs=pl.BlockSpec((1, 2, rows, width), lambda i: (i, 0, 0, 0)),
        out_shape=jax.ShapeDtypeStruct((count, 2, rows, width), BF),
        cost_estimate=small_cost(),
    )(inputs, cotangent, gain.reshape(1, -1), bias.reshape(1, -1))


def dot(left, right, left_dim=1, right_dim=0):
    return lax.dot_general(
        left, right, (((left_dim,), (right_dim,)), ((), ())), preferred_element_type=F32
    )


def after(values, *gates):
    return lax.optimization_barrier((values, gates))[0]


def small_cost():
    return pl.CostEstimate(flops=1 << 20, bytes_accessed=1 << 16, transcendentals=0)


def whole(shape):
    return pl.BlockSpec(shape, lambda *at: (0,) * len(shape))


def gelu_both(values):
    scale, cubic = math.sqrt(2.0 / math.pi), 0.044715
    square = values * values
    tanh = jnp.tanh(scale * values * (1.0 + cubic * square))
    half = 0.5 * (1.0 + tanh)
    slope = half + 0.5 * scale * values * (1.0 - tanh * tanh) * (1.0 + 3.0 * cubic * square)
    return values * half, slope


def ff_kernel(
    units_ref, own_ref, other_ref, w_in_ref, b_in_ref, w_out_ref,
    first_ref, second_ref, act_ref, inner_ref, bias_ref,
    normed, grad, normed_turned,
):
    step = pl.program_id(0)
    count, _, rows, _ = own_ref.shape

    @pl.when(step == 0)
    def _():
        for place, ref in enumerate((own_ref, other_ref)):
            for i in range(count):
                at = slice((place * count + i) * rows, (place * count + i + 1) * rows)
                normed[at] = ref[i, 0]
                grad[at] = ref[i, 1]
        normed_turned[...] = normed[...].T

    act, slope = gelu_both(dot(normed[...], w_in_ref[...]) + b_in_ref[...])
    act = act.astype(BF)
    act_ref[...] = act
    grad_inner = (dot(grad[...], w_out_ref[...], 1, 1) * slope).astype(BF)
    inner_ref[...] = grad_inner
    bias_ref[...] = jnp.sum(grad_inner.astype(F32), axis=0, keepdims=True)
    units = act.shape[1]
    grad_w_out = dot(act, grad[...], 0, 0).astype(BF)
    grad_w_in = dot(normed_turned[...], grad_inner).astype(BF)

    def store(ref):
        ref[:units] = grad_w_out
        ref[units:, :units] = grad_w_in[:units]
        ref[units:, units:] = grad_w_in[units:]

    pl.when(step == 0)(lambda: store(first_ref))
    pl.when(step == 1)(lambda: store(second_ref))


def feed_forward(units, own, other, w_in, b_in, w_out):
    tokens, width = own.shape[0] * own.shape[2], own.shape[3]
    size = w_in.shape[1] // 8
    block = pl.BlockSpec((2 * tokens, size), lambda step, units: (0, step))
    return pl.pallas_call(
        ff_kernel,
        grid_spec=pltpu.PrefetchScalarGridSpec(
            num_scalar_prefetch=1,
            grid=(2,),
            in_specs=[whole(own.shape)] * 2
            + [
                pl.BlockSpec((width, size), lambda step, units: (0, units[step])),
                pl.BlockSpec((1, size), lambda step, units: (0, units[step])),
                pl.BlockSpec((size, width), lambda step, units: (units[step], 0)),
            ],
            out_specs=[whole((2 * size, width))] * 2
            + [block, block, pl.BlockSpec((1, size), lambda step, units: (0, step))],
            scratch_shapes=[
                pltpu.VMEM((2 * tokens, width), BF),
                pltpu.VMEM((2 * tokens, width), BF),
                pltpu.VMEM((width, 2 * tokens), BF),
            ],
        ),
        out_shape=[jax.ShapeDtypeStruct((2 * size, width), BF)] * 2
        + [jax.ShapeDtypeStruct((2 * tokens, 2 * size), BF)] * 2
        + [jax.ShapeDtypeStruct((1, 2 * size), F32)],
        compiler_params=pltpu.CompilerParams(vmem_limit_bytes=56 << 20),
        cost_estimate=small_cost(),
    )(units, own, other, w_in, b_in, w_out)


def ff_late_kernel(
    units_ref, own_ref, other_ref, act_ref, inner_ref, w_in_ref, b_in_ref, w_out_ref,
    first_ref, second_ref, bias_ref, kept, sent,
    normed, grad, normed_turned, out_sum, back_sum,
):
    step = pl.program_id(0)
    count, _, rows, _ = own_ref.shape
    tokens = count * rows
    size = w_in_ref.shape[1]

    @pl.when(step == 0)
    def _():
        for place, ref in enumerate((own_ref, other_ref)):
            for i in range(count):
                at = slice((place * count + i) * rows, (place * count + i + 1) * rows)
                normed[at] = ref[i, 0]
                grad[at] = ref[i, 1]
        normed_turned[...] = normed[...].T

    def add(act, grad_inner):
        out = dot(act, w_out_ref[...])
        back = dot(grad_inner, w_in_ref[...], 1, 1)

        @pl.when(step == 0)
        def _():
            out_sum[...] = out
            back_sum[...] = back

        @pl.when(step > 0)
        def _():
            out_sum[...] += out
            back_sum[...] += back

    @pl.when(step < 2)
    def _():
        act, slope = gelu_both(dot(normed[...], w_in_ref[...]) + b_in_ref[...])
        act = act.astype(BF)
        grad_inner = (dot(grad[...], w_out_ref[...], 1, 1) * slope).astype(BF)
        bias_ref[...] = jnp.sum(grad_inner.astype(F32), axis=0, keepdims=True)
        grad_w_out = dot(act, grad[...], 0, 0).astype(BF)
        grad_w_in = dot(normed_turned[...], grad_inner).astype(BF)

        def store(ref):
            ref[:size] = grad_w_out
            ref[size:, :size] = grad_w_in[:size]
            ref[size:, size:] = grad_w_in[size:]

        pl.when(step == 0)(lambda: store(first_ref))
        pl.when(step == 1)(lambda: store(second_ref))
        add(act, grad_inner)

    for i in range(2):

        @pl.when(step == 2 + i)
        def _():
            cols = slice(i * size, (i + 1) * size)
            add(act_ref[:, cols], inner_ref[:, cols])

    @pl.when(step == 3)
    def _():
        for i, sums in enumerate((out_sum, back_sum)):
            kept[i] = sums[:tokens]
            sent[i] = sums[tokens:].astype(BF)


def feed_forward_late(units, own, other, w_in, b_in, w_out, act, inner):
    tokens, width = own.shape[0] * own.shape[2], own.shape[3]
    size = w_in.shape[1] // 8

    def once(shape):
        return pl.BlockSpec(
            shape, lambda *at: (0,) * len(shape), pipeline_mode=pl.Buffered(1)
        )

    return pl.pallas_call(
        ff_late_kernel,
        grid_spec=pltpu.PrefetchScalarGridSpec(
            num_scalar_prefetch=1,
            grid=(4,),
            in_specs=[once(own.shape)] * 2
            + [once(act.shape)] * 2
            + [
                pl.BlockSpec((width, size), lambda step, units: (0, units[step])),
                pl.BlockSpec((1, size), lambda step, units: (0, units[step])),
                pl.BlockSpec((size, width), lambda step, units: (units[step], 0)),
            ],
            out_specs=[whole((2 * size, width))] * 2
            + [pl.BlockSpec((1, size), lambda step, units: (0, jnp.minimum(step, 1)))]
            + [whole((2, tokens, width))] * 2,
            scratch_shapes=[
                pltpu.VMEM((2 * tokens, width), BF),
                pltpu.VMEM((2 * tokens, width), BF),
                pltpu.VMEM((width, 2 * tokens), BF),
            ]
            + [pltpu.VMEM((2 * tokens, width), F32)] * 2,
        ),
        out_shape=[jax.ShapeDtypeStruct((2 * size, width), BF)] * 2
        + [
            jax.ShapeDtypeStruct((1, 2 * size), F32),
            jax.ShapeDtypeStruct((2, tokens, width), F32),
            jax.ShapeDtypeStruct((2, tokens, width), BF),
        ],
        compiler_params=pltpu.CompilerParams(vmem_limit_bytes=62 << 20),
        cost_estimate=small_cost(),
    )(units, own, other, act, inner, w_in, b_in, w_out)


def attend(bound, query, key, value, grad, rotate_back, scratch, block):
    k_turned, v_turned, mixed_turned, gq_turned, gk_sum, gv_sum = scratch
    count, lanes = query.shape
    k_turned[...] = key.T
    v_turned[...] = value.T
    g_turned = grad.T
    gk_sum[...] = jnp.zeros_like(gk_sum)
    gv_sum[...] = jnp.zeros_like(gv_sum)
    lane = lax.broadcasted_iota(jnp.int32, (count, lanes), 1)
    for head in range(lanes // HEAD_DIM):
        cols = slice(head * HEAD_DIM, (head + 1) * HEAD_DIM)
        mine = (lane >= head * HEAD_DIM) & (lane < (head + 1) * HEAD_DIM)
        q_head = jnp.where(mine, query, jnp.zeros_like(query))
        g_head = jnp.where(mine, grad, jnp.zeros_like(grad))
        for start in range(0, count, block):
            seen = start + block
            rows = slice(start, seen)
            scores = dot(key[:seen], q_head[rows], 1, 1)
            at_key = lax.broadcasted_iota(jnp.int32, (seen, block), 0)
            at_query = lax.broadcasted_iota(jnp.int32, (1, block), 1) + start
            lowest = jnp.where(at_query >= bound, bound, 0)
            scores = jnp.where((at_key <= at_query) & (at_key >= lowest), scores, -1e30)
            probs = jnp.exp(scores - jnp.max(scores, axis=0, keepdims=True))
            probs = probs * (1.0 / jnp.sum(probs, axis=0, keepdims=True))
            probs_low = probs.astype(BF)
            grad_probs = dot(value[:seen], g_head[rows], 1, 1)
            mixed = dot(v_turned[cols, :seen], probs_low)
            mixed_turned[cols, rows] = mixed
            row_dot = jnp.sum(mixed * g_turned[cols, rows].astype(F32), axis=0, keepdims=True)
            grad_scores = (probs * (grad_probs - row_dot)).astype(BF)
            gq_turned[cols, rows] = dot(k_turned[cols, :seen], grad_scores)
            gv_sum[:seen, :] += dot(probs_low, g_head[rows])
            gk_sum[:seen, :] += dot(grad_scores, q_head[rows])
    grad_query = (gq_turned[...].T * HEAD_DIM ** -0.5).astype(BF).astype(F32)
    return (
        rotate_back(grad_query).astype(BF),
        rotate_back(gk_sum[...].astype(BF).astype(F32)).astype(BF),
        gv_sum[...].astype(BF),
    )


def heads_kernel(
    scalars_ref, held, there, w_q_ref, w_k_ref, w_v_ref, w_p_ref, cos_ref, ahead_ref, behind_ref,
    mixed_ref, grads_ref, *rest, pairs, block,
):
    sums, (normed_ref, grad_ref, normed_turned), scratch = (
        rest[:pairs], rest[pairs : pairs + 3], rest[pairs + 3 :]
    )
    step = pl.program_id(0)
    bound, core = scalars_ref[0], scalars_ref[1]
    count, width = normed_ref.shape
    chunks, _, rows, _ = held.shape
    lanes = w_q_ref.shape[1]
    cosine, ahead, behind = cos_ref[...], ahead_ref[...], behind_ref[...]

    def at(index):
        return pl.ds(pl.multiple_of(index * rows, rows), rows)

    def rotate(values):
        return (
            values * cosine
            + pltpu.roll(values, lanes - 1, 1) * ahead
            + pltpu.roll(values, 1, 1) * behind
        )

    def rotate_back(grads):
        return (
            grads * cosine
            + pltpu.roll(grads * ahead, 1, 1)
            + pltpu.roll(grads * behind, lanes - 1, 1)
        )

    @pl.when(step == 0)
    def _():
        for i in range(chunks):
            mine, other = at(2 * i + core), at(2 * i + 1 - core)
            normed_ref[mine, :] = held[i, 0]
            normed_ref[other, :] = there[i, 0]
            grad_ref[mine, :] = held[i, 1]
            grad_ref[other, :] = there[i, 1]
        normed_turned[...] = normed_ref[...].T

    weights = jnp.concatenate([w_q_ref[...], w_k_ref[...], w_v_ref[...]], axis=1)
    raw = dot(normed_ref[...], weights)
    query = (rotate(raw[:, :lanes]).astype(BF).astype(F32) * HEAD_DIM ** -0.5).astype(BF)
    key = rotate(raw[:, lanes : 2 * lanes]).astype(BF)
    value = raw[:, 2 * lanes :].astype(BF)
    grad_mixed = dot(grad_ref[...], w_p_ref[...], 1, 1).astype(BF)
    parts = attend(bound, query, key, value, grad_mixed, rotate_back, scratch, block)
    mixed_turned = scratch[2][...].astype(BF)
    mixed_ref[...] = mixed_turned.T
    grads = jnp.concatenate(parts, axis=1)
    grads_ref[...] = grads
    grad_weights = dot(normed_turned[...], grads).astype(BF)
    grad_proj = dot(mixed_turned, grad_ref[...]).astype(BF)

    def store(ref):
        ref[:lanes] = grad_proj
        for i in range(3):
            for j in range(width // lanes):
                ref[(i + 1) * lanes : (i + 2) * lanes, j * lanes : (j + 1) * lanes] = grad_weights[
                    j * lanes : (j + 1) * lanes, i * lanes : (i + 1) * lanes
                ]

    for i in range(pairs):
        pl.when(step == i)(functools.partial(store, sums[i]))


def attention(scalars, pairs, window, w_query, w_key, w_value, w_proj, turns):
    chunks, _, rows, width = window[0].shape
    count = 2 * chunks * rows
    cols = pl.BlockSpec((width, LANES), lambda step, s: (0, s[2 + step]))
    sums = jax.ShapeDtypeStruct((4 * LANES, width), BF)
    return pl.pallas_call(
        functools.partial(heads_kernel, pairs=pairs, block=512),
        grid_spec=pltpu.PrefetchScalarGridSpec(
            num_scalar_prefetch=1,
            grid=(pairs,),
            in_specs=[whole(window[0].shape)] * 2
            + [cols] * 3
            + [pl.BlockSpec((LANES, width), lambda step, s: (s[2 + step], 0))]
            + [whole((count, LANES))] * 3,
            out_specs=[
                pl.BlockSpec((count, LANES), lambda step, s: (0, step)),
                pl.BlockSpec((count, 3 * LANES), lambda step, s: (0, step)),
            ]
            + [whole(sums.shape)] * pairs,
            scratch_shapes=[
                pltpu.VMEM((count, width), BF),
                pltpu.VMEM((count, width), BF),
                pltpu.VMEM((width, count), BF),
            ]
            + [pltpu.VMEM((LANES, count), BF)] * 2
            + [pltpu.VMEM((LANES, count), F32)] * 2
            + [pltpu.VMEM((count, LANES), F32)] * 2,
        ),
        out_shape=[
            jax.ShapeDtypeStruct((count, pairs * LANES), BF),
            jax.ShapeDtypeStruct((count, 3 * pairs * LANES), BF),
        ]
        + [sums] * pairs,
        compiler_params=pltpu.CompilerParams(vmem_limit_bytes=60 << 20),
        cost_estimate=small_cost(),
    )(scalars, *window, w_query, w_key, w_value, w_proj, *turns)


def heads_ends_kernel(
    scalars_ref, *refs, calls,
):
    tensors, (w_q, w_k, w_v, w_p, kept, sent, out_sum, back_sum) = refs[: 2 * calls], refs[2 * calls :]
    step = pl.program_id(0)
    core = scalars_ref[0]
    chunks, _, rows, _ = kept.shape
    first = 0
    for call in range(calls):
        mixed, grads = tensors[2 * call : 2 * call + 2]
        for i in range(mixed.shape[1] // LANES):

            @pl.when(step == first + i)
            def _():
                weights = jnp.concatenate([w_q[...], w_k[...], w_v[...]], axis=1)
                out = dot(mixed[:, i * LANES : (i + 1) * LANES], w_p[...])
                back = dot(grads[:, 3 * i * LANES : 3 * (i + 1) * LANES], weights, 1, 1)
                if first + i == 0:
                    out_sum[...] = out
                    back_sum[...] = back
                else:
                    out_sum[...] += out
                    back_sum[...] += back

        first += mixed.shape[1] // LANES

    @pl.when(step == first - 1)
    def _():
        for i in range(chunks):
            for j, sums in enumerate((out_sum, back_sum)):
                mine = pl.ds(pl.multiple_of((2 * i + core) * rows, rows), rows)
                other = pl.ds(pl.multiple_of((2 * i + 1 - core) * rows, rows), rows)
                kept[i, j] = sums[mine, :]
                sent[i, j] = sums[other, :].astype(BF)


def heads_ends(scalars, parts, shape, w_query, w_key, w_value, w_proj):
    count, width = parts[0][0].shape[0], w_query.shape[0]
    pairs = sum(mixed.shape[1] for mixed, _ in parts) // LANES
    tensors = [tensor for part in parts for tensor in part]
    cols = pl.BlockSpec((width, LANES), lambda step, s: (0, s[1 + step]))
    return pl.pallas_call(
        functools.partial(heads_ends_kernel, calls=len(parts)),
        grid_spec=pltpu.PrefetchScalarGridSpec(
            num_scalar_prefetch=1,
            grid=(pairs,),
            in_specs=[whole(tensor.shape) for tensor in tensors]
            + [cols] * 3
            + [pl.BlockSpec((LANES, width), lambda step, s: (s[1 + step], 0))],
            out_specs=[whole(shape)] * 2,
            scratch_shapes=[pltpu.VMEM((count, width), F32)] * 2,
        ),
        out_shape=[jax.ShapeDtypeStruct(shape, F32), jax.ShapeDtypeStruct(shape, BF)],
        compiler_params=pltpu.CompilerParams(vmem_limit_bytes=60 << 20),
        cost_estimate=small_cost(),
    )(scalars, *tensors, w_query, w_key, w_value, w_proj)


def place_ff_kernel(out_ref, in_ref, w_out_ref, w_in_ref):
    size = w_in_ref.shape[2]
    w_out_ref[...] = out_ref[0].astype(F32)
    both = in_ref[0].astype(F32)
    w_in_ref[0] = both[:, :size]
    w_in_ref[1] = both[:, size:]


def device_of(core, index, steps):
    at = {"x": 0, "y": 0}
    for place, (axis, bit) in enumerate(steps):
        at[axis] = at[axis] + (index // 2 ** (len(steps) - 1 - place)) % 2 * 2**bit
    return (at["x"] * lax.axis_size("y") + at["y"]) * 2 + core


def place_ff(parts, orders):
    devices, held, width = parts.shape
    held, size = held // 2, width // 2
    rows = min(size, held)
    chunks = size // rows

    def split(step):
        return step // (4 * chunks), step // (2 * chunks) % 2, step // chunks % 2, step % chunks

    def source(step, of_in):
        core, chain, first, chunk = split(step)
        row = of_in * size + chunk * rows
        index = first * (width // held) + row // held
        a_side, b_side = (device_of(core, index, steps) for steps in orders)
        return (jnp.where(chain == 0, a_side, b_side), (chain * held + row % held) // rows, 0)

    def block_of(step):
        core, chain, first, chunk = split(step)
        return core * 4 + chain * 2 + first, chunk

    return pl.pallas_call(
        place_ff_kernel,
        grid=(8 * chunks,),
        in_specs=[
            pl.BlockSpec((1, rows, width), lambda step: source(step, 0)),
            pl.BlockSpec((1, rows, width), lambda step: source(step, 1)),
        ],
        out_specs=[
            pl.BlockSpec(
                (rows, width), lambda step: (block_of(step)[0] * chunks + block_of(step)[1], 0)
            ),
            pl.BlockSpec((2, rows, size), lambda step: (0, block_of(step)[1], block_of(step)[0])),
        ],
        out_shape=[
            jax.ShapeDtypeStruct((8 * size, width), F32),
            jax.ShapeDtypeStruct((2, size, 8 * size), F32),
        ],
        compiler_params=pltpu.CompilerParams(vmem_limit_bytes=60 << 20),
        cost_estimate=small_cost(),
    )(parts, parts)


def place_heads_kernel(pairs_ref, a_ref, b_ref, c_ref, d_ref, *rest):
    q_out, k_out, v_out, p_out = rest[-4:]
    lanes, width = p_out.shape
    for index, ref in enumerate((a_ref, b_ref, c_ref, d_ref)):

        @pl.when(pl.program_id(0) == index)
        def _():
            p_out[...] = ref[:lanes].astype(F32)
            for i, out in enumerate((q_out, k_out, v_out)):
                for j in range(width // lanes):
                    out[j * lanes : (j + 1) * lanes, :] = ref[
                        (i + 1) * lanes : (i + 2) * lanes, j * lanes : (j + 1) * lanes
                    ].astype(F32)


def place_heads(pairs, sums, filled=()):
    width = sums[0].shape[1]
    cols = pl.BlockSpec((width, LANES), lambda step, pairs: (0, pairs[step]))
    return pl.pallas_call(
        place_heads_kernel,
        grid_spec=pltpu.PrefetchScalarGridSpec(
            num_scalar_prefetch=1,
            grid=(4,),
            in_specs=[whole(sums[0].shape)] * 4
            + [pl.BlockSpec(memory_space=pl.ANY)] * len(filled),
            out_specs=[cols] * 3
            + [pl.BlockSpec((LANES, width), lambda step, pairs: (pairs[step], 0))],
        ),
        out_shape=[jax.ShapeDtypeStruct((width, width), F32)] * 4,
        input_output_aliases={5 + i: i for i in range(len(filled))},
        compiler_params=pltpu.CompilerParams(vmem_limit_bytes=60 << 20),
        cost_estimate=small_cost(),
    )(pairs, *sums, *filled)


def swap(values, axis, bits):
    return lax.ppermute(
        values, axis, [(i, i ^ bits) for i in range(lax.axis_size(axis))]
    )


def cross(values):
    return values, lax.ppermute(values, ("x", "core"), [(1, 2), (2, 1)])


def crossed(pair):
    return jnp.where(lax.axis_index("x") == lax.axis_index("core"), *pair)


def trade_z(cubes):
    return lax.all_to_all(crossed(cubes), "z", split_axis=0, concat_axis=0, tiled=True)


def trade_parts(cubes, z):
    def entry(k):
        at = [lax.dynamic_index_in_dim(cube, z ^ k, 0, keepdims=True) for cube in cubes]
        return crossed(at)

    count = cubes[0].shape[0]
    return [entry(0)] + [swap(entry(k), "z", k) for k in range(1, count)]


def land_kernel(z_ref, *refs):
    for k in range(len(refs) - 1):

        @pl.when(pl.program_id(0) == k)
        def _():
            refs[-1][...] = refs[k][...]


def landed(entries, z):
    count = len(entries)
    shape = entries[0].shape
    return pl.pallas_call(
        land_kernel,
        grid_spec=pltpu.PrefetchScalarGridSpec(
            num_scalar_prefetch=1,
            grid=(count,),
            in_specs=[whole(shape)] * count,
            out_specs=pl.BlockSpec(shape, lambda k, z: (z[0] ^ k, 0, 0, 0)),
        ),
        out_shape=jax.ShapeDtypeStruct((count,) + shape[1:], BF),
        cost_estimate=small_cost(),
    )(z.reshape(1), *entries)


def ordered(first_is_own, own, other, axis):
    return jnp.where(
        first_is_own,
        jnp.concatenate([own, other], axis=axis),
        jnp.concatenate([other, own], axis=axis),
    )


def steps_of(order):
    found = []
    for letter in order:
        bits = [(letter.lower(), b) for b in range(lax.axis_size(letter.lower()).bit_length() - 1)]
        found += bits[::-1] if letter == "Z" else bits
    return found


def bit_of(step):
    axis, bit = step
    return (lax.axis_index(axis) >> bit) & 1


def trade(values, step):
    axis, bit = step
    return swap(values, axis, 1 << bit)


def sum_kernel(at_ref, *refs, counts):
    first = 0
    for count, out in zip(counts, refs[sum(counts) :]):
        out[...] = sum(ref[...].astype(F32) for ref in refs[first : first + count]).astype(BF)
        first += count


def sums_of(chains, half):
    if half < 64:
        return [rows_sum(terms, half) for terms in chains]
    blocks = 4 if half >= 256 else 1
    width = chains[0][0][0].shape[1]
    shape = (half // blocks, width)
    flat = [term for terms in chains for term in terms]

    def spec(index):
        return pl.BlockSpec(shape, lambda i, at: (at[index] * blocks + i, 0))

    starts = jnp.stack([jnp.asarray(at // half, jnp.int32) for _, at in flat])
    return pl.pallas_call(
        functools.partial(sum_kernel, counts=[len(terms) for terms in chains]),
        grid_spec=pltpu.PrefetchScalarGridSpec(
            num_scalar_prefetch=1,
            grid=(blocks,),
            in_specs=[spec(index) for index in range(len(flat))],
            out_specs=[pl.BlockSpec(shape, lambda i, at: (i, 0))] * len(chains),
        ),
        out_shape=[jax.ShapeDtypeStruct((half, width), BF)] * len(chains),
        cost_estimate=small_cost(),
    )(starts, *[array for array, _ in flat])


def spread(values, *axes):
    steps = steps_of(axes)
    if len(steps) != 2:
        for step in steps[:-1]:
            values = values + trade(values, step)
        return [values, trade(values, steps[-1])]
    if len(axes) == 1:
        both = swap(values, axes[0], 3)
    else:
        n = lax.axis_size(axes[1])
        pairs = [(i, (i // n ^ 1) * n + (i % n ^ 1)) for i in range(2 * n)]
        both = lax.ppermute(values, axes, pairs)
    return [values, trade(values, steps[0]), trade(values, steps[1]), both]


def total(parts):
    if len(parts) == 2:
        return parts[0] + parts[1]
    return (parts[0] + parts[1]) + (parts[2] + parts[3])


def reduce_both(chains, steps):
    half = chains[0][-1][0].shape[0] // 2
    owns = [bit_of(step) for step in steps]
    sent = sums_of(
        [[(array, at + (1 - own) * half) for array, at in terms] for terms, own in zip(chains, owns)],
        half,
    )
    kept = [
        [(array, at + own * half) for array, at in terms] + [(trade(went, step), 0)]
        for terms, own, went, step in zip(chains, owns, sent, steps)
    ]
    return kept, sent


def rows_sum(terms, rows):
    parts = [lax.dynamic_slice_in_dim(array, at, rows, 0) for array, at in terms]
    return sum(part.astype(F32) for part in parts).astype(BF)


def summed(chains):
    return sums_of(chains, chains[0][-1][0].shape[0])


def join(share, got, step):
    return ordered(bit_of(step) == 0, share, got, 0)


def gather_step(share, step):
    return join(share, trade(share, step), step)


def body(
    inputs,
    cotangent,
    offsets,
    end_flags,
    ln_gain,
    ln_bias,
    w_query,
    w_key,
    w_value,
    w_proj,
    w_in,
    b_in,
    w_out,
    b_out,
):
    count, rows, width = inputs.shape
    hidden = w_in.shape[1]
    tokens = count * rows
    assert count == lax.axis_size("z")
    z, x, c = (lax.axis_index(axis) for axis in ("z", "x", "core"))
    first_a, first_b = steps_of("x"), steps_of("y")[:1]
    near_a, near_b = steps_of("y"), steps_of("y")[1:] + steps_of("x")
    rest_a, rest_b = near_a + steps_of("z"), near_b + steps_of("Z")
    own_a, own_b = bit_of(first_a[0]), bit_of(first_b[0])
    core = c * 4
    sent = jnp.stack([core + 1 - own_a, core + 3 - own_b]).astype(jnp.int32)
    kept = jnp.stack([core + own_a, core + 2 + own_b]).astype(jnp.int32)

    bounds = jnp.where(end_flags == 1, offsets, 0).astype(F32)
    bounds = jnp.where(x == c, bounds, swap(bounds, "core", 1)).astype(jnp.int32)
    bound = lax.dynamic_index_in_dim(bounds, z, 0, keepdims=False)
    turns = tables(2 * count * rows)

    pair = norm_pair(inputs, cotangent, ln_gain, ln_bias)
    pair_other = swap(pair, "core", 1)
    pair_cross = cross(pair)

    ff_args = (pair, pair_other, w_in, b_in.reshape(1, -1), w_out)
    a_sent, b_sent, act, inner, bias = feed_forward(sent, *ff_args)
    a_got, b_got = trade(a_sent, first_a[0]), trade(b_sent, first_b[0])
    entries = trade_parts(after(pair_cross, bias), z)
    a_kept, b_kept, bias_late, ff_kept, ff_sent = feed_forward_late(
        after(jnp.concatenate([kept, sent]), bias, entries[0]), *ff_args, act, inner
    )

    steps = list(zip(rest_a, rest_b))
    a_got, b_got = after((a_got, b_got), ff_kept)
    ff_terms, went = reduce_both([[(a_kept, 0), (a_got, 0)], [(b_kept, 0), (b_got, 0)]], steps[0])
    held = landed(after(entries, went), z)
    there = swap(held, "core", 1)
    attn_args = ((held, there), w_query, w_key, w_value, w_proj, turns)

    def scalars(*values):
        return jnp.stack([jnp.asarray(value, jnp.int32) for value in values])

    *parts_1, ha_sent = attention(scalars(bound, c, sent[0]), 1, *attn_args)
    ff_terms, ha_sent, ff_sent = after((ff_terms, ha_sent, ff_sent), parts_1)
    ff_terms, went = reduce_both(ff_terms, steps[1])
    ff_other = swap(ff_sent, "core", 1)
    ha_got = trade(ha_sent, first_a[0])
    *parts_2, hb_sent, ha_kept = attention(
        after(scalars(bound, c, sent[1], kept[0]), went), 2, *attn_args
    )
    ff_terms, hb_sent, ff_other = after((ff_terms, hb_sent, ff_other), parts_2)
    ff_terms, went = reduce_both(ff_terms, steps[2])
    hb_got = trade(hb_sent, first_b[0])
    *parts_3, hb_kept = attention(after(scalars(bound, c, kept[1]), went, ff_other), 1, *attn_args)
    ff_terms = after(ff_terms, hb_kept)
    for step in steps[3:]:
        ff_terms, _ = reduce_both(ff_terms, step)
    far, near = steps[len(near_a) :], steps[: len(near_a)]
    ff_sums = summed(ff_terms)

    def grown(sums, step):
        return [gather_step(share, one) for share, one in zip(sums, step)]

    got = [trade(sums, step) for sums, step in zip(ff_sums, far[-1])]
    terms = after([[(ha_kept, 0), (ha_got, 0)], [(hb_kept, 0), (hb_got, 0)]], ff_sums)
    terms, went = reduce_both(terms, steps[0])
    heads_kept, heads_sent = heads_ends(
        after(scalars(c, sent[0], sent[1], kept[0], kept[1]), went),
        (parts_1, parts_2, parts_3), held.shape, w_query, w_key, w_value, w_proj,
    )
    got, terms, heads_sent = after((got, terms, heads_sent), heads_kept)
    for after_step, step in zip(far[:0:-1], far[-2::-1]):
        ff_sums = [join(*one) for one in zip(ff_sums, got, after_step)]
        got = [trade(sums, one) for sums, one in zip(ff_sums, step)]
    heads_other = swap(after(heads_sent, ff_sums), "core", 1)
    out_cross, back_cross = (
        cross((heads_kept[:, i] + heads_other[:, i].astype(F32)).astype(BF)) for i in range(2)
    )
    got = after(got, out_cross, back_cross)
    ff_sums = [join(*one) for one in zip(ff_sums, got, far[0])]
    share = jnp.concatenate(ff_sums, axis=0)
    ff_parts = lax.all_gather(share, ("x", "y", "core"), axis=0, tiled=False)
    terms, back_cross = after((terms, back_cross), share)
    terms, _ = reduce_both(terms, steps[1])
    terms, back_cross = after((terms, back_cross))
    heads_back = trade_z(back_cross)
    for step in steps[2:]:
        terms, _ = reduce_both(terms, step)
    sums = summed(after(terms))
    got = [trade(share, one) for share, one in zip(sums, far[-1])]
    heads_back = after(heads_back, sums)

    ff = (ff_kept + ff_other.astype(F32)).reshape(2, count, rows, width)
    full_in, grad_full = inputs.astype(F32), cotangent.astype(F32)
    _, norm_back = jax.vjp(layernorm, full_in, ln_gain, ln_bias)
    grad_flat, grad_ln_gain, grad_ln_bias = norm_back(ff[1] + heads_back.astype(F32))
    grad_inputs = grad_full + grad_flat

    grad_b_in = jnp.zeros((8, hidden // 8), F32)
    for units, rows_of in ((sent, bias), (kept, bias_late)):
        for i in range(2):
            part = rows_of[:, i * hidden // 8 : (i + 1) * hidden // 8]
            grad_b_in = lax.dynamic_update_slice_in_dim(grad_b_in, part, units[i], 0)
    small = jnp.concatenate(
        [grad_ln_gain, grad_ln_bias, grad_b_in.reshape(-1), jnp.sum(grad_full, axis=(0, 1))]
    ).reshape(-1, LANES)
    sums = [join(*one) for one in zip(sums, after(got, small), far[-1])]
    for step in far[-2::-1]:
        small = after(small, sums)
        sums = grown(sums, step)
    small = total(spread(small, "z"))
    small = total(spread(small, "core"))
    heads_out = trade_z(after(out_cross, sums, small))

    sums, ff_parts, small = after((sums, ff_parts, small))
    small = spread(small, "x", "y")
    for step in near[:0:-1]:
        sums = grown(sums, step)
    got = [trade(share, step) for share, step in zip(sums, near[0])]
    got, small = after((got, small))
    sums = [join(*one) for one in zip(sums, got, near[0])]
    distant = [trade(share, step[0]) for share, step in zip(sums, (first_a, first_b))]
    other = [swap(share, "core", 1) for share in sums]
    orders = (first_a + near_a, first_b + near_b)
    sum_w_out, sum_w_in = place_ff(after(ff_parts, sums), orders)
    heads_out = after(heads_out, sum_w_out).astype(F32)
    outputs = (full_in + heads_out + ff[0] + b_out).astype(BF)
    across = jnp.stack([4 - 2 * core] * 2)
    filled = place_heads(
        jnp.concatenate([kept, kept + across]), sums + after(other, sum_w_out)
    )
    distant = after(distant, filled)
    sum_query, sum_key, sum_value, sum_proj = place_heads(
        jnp.concatenate([sent, sent + across]),
        distant + [swap(share, "core", 1) for share in distant],
        filled,
    )
    small = total(small)
    sum_ln_gain, sum_ln_bias, sum_b_in, sum_b_out = jnp.split(
        small.reshape(-1), [width, 2 * width, 2 * width + hidden]
    )
    return (
        outputs,
        grad_inputs,
        sum_ln_gain,
        sum_ln_bias,
        sum_query,
        sum_key,
        sum_value,
        sum_proj,
        sum_w_in.reshape(width, hidden),
        sum_b_in,
        sum_w_out,
        sum_b_out,
    )


def solution(mesh):
    n_seq, n_win = mesh.devices.shape
    fine = jax.sharding.Mesh(
        mesh.devices.reshape(n_seq // 2, 2, n_win // 2, 2), ("z", "x", "y", "core")
    )
    win, seq = ("y", "core"), ("z", "x")
    cube = P(win, seq, None)
    return jax.shard_map(
        body,
        mesh=fine,
        in_specs=(cube, cube, P(win), P(win)) + (P(),) * 10,
        out_specs=(cube, cube) + (P(),) * 10,
        check_vma=False,
    )
```
